512 devices in a mesh: dom: 256 (over x, z, y), band: 2 (over core).
Axes of the slice: x: 4, y: 4, z: 16, core: 2. Of those that a mesh axis runs over, the one named last changes fastest.
Arguments:
- block: bfloat16 [128, 262144], P('band', 'dom')
- cell_nodes: int32 [8192, 125], P('dom'), may hold values from 0 to 1535, as said below
- send_lists: int32 [256, 2, 256], P('dom'), may hold values from 0 to 1023, as said below
- cell_matrix: bfloat16 [125, 125], replicated
- cell_scale: float32 [8192], P('dom'), may hold values from 0.5 to 2
- potential: float32 [262144], P('dom'), may hold values from -1 to 0.5
Outputs:
- ortho_block: float32 [128, 262144], P(None, ('dom', 'band'))
- projected: float32 [128, 128], replicated
The draws below stay inside these ranges and needn't reach their ends.
Inputs may be any that keep to these rules, and one draw needn't show every extreme that they name: `cell_nodes`: entries below 1024 name the partition's own nodes, from 1024 to 1279 the ghost slots filled by the left neighbour, and the rest those filled by the right neighbour. The first partition's cells use no left slots and the last partition's no right slots; how many slots are used differs from partition to partition. `send_lists`: node indices in the numbering of the sending partition; a node may stand in a list more than once.
All inputs are finite; a program needn't handle non-finite values.
Results may differ from the reference program's by a relative error of at most 0.013.
Values may be sent and summed in bfloat16 or wider, within the bound.
No kernel may reach another device: no remote copies, remote signals or barrier semaphores. Data moves between devices by JAX's collectives and lax.ppermute only.
A program may use at most 64 MiB of HBM per device.

```python
import math
import jax
import jax.numpy as jnp
from jax import lax

STATES = 128
CELL_NODES = 125
NODE_DEV = 1024
CELL_DEV = 32
GHOSTS = 256
NODES = 262144
CELLS = 8192


def draw_block(key, part):
    key = jax.random.fold_in(key, 11)
    key_cols, key_rough, key_bulk = jax.random.split(key, 3)
    column_scale = jnp.exp(jax.random.uniform(key_cols, (STATES, 1), jnp.float32) * jnp.log(10.0))
    position = jnp.arange(NODES, dtype=jnp.float32)[None, :] / NODES
    node_rough = jnp.exp(jax.random.uniform(key_rough, (1, NODES), jnp.float32) * jnp.log(10.0))
    values = jax.random.normal(key_bulk, (STATES, NODES), jnp.float32)
    scaled = values * column_scale * node_rough * (1.0 + 2.0 * position) / 8.0
    return scaled.astype(jnp.bfloat16)


def draw_cell_matrix(key, part):
    key = jax.random.fold_in(key, 13)
    key_off, key_diag = jax.random.split(key, 2)
    offdiag = 0.01 * jax.random.normal(key_off, (CELL_NODES, CELL_NODES), jnp.float32)
    diagonal = jax.random.uniform(key_diag, (CELL_NODES,), jnp.float32, 0.04, 0.12)
    matrix = offdiag + offdiag.T + jnp.diag(diagonal)
    return matrix.astype(jnp.bfloat16)


def draw_cell_nodes(key, part):
    key = jax.random.fold_in(key, 5)
    domains = CELLS // CELL_DEV
    key_left, key_right, key_pick = jax.random.split(key, 3)
    left_used = jax.random.randint(key_left, (domains,), GHOSTS // 4, GHOSTS + 1)
    left_used = left_used.at[1].set(GHOSTS).at[0].set(0)
    right_used = jax.random.randint(key_right, (domains,), GHOSTS // 4, GHOSTS + 1)
    right_used = right_used.at[0].set(GHOSTS).at[domains - 1].set(0)
    span_size = (NODE_DEV + left_used + right_used)[:, None, None]
    raw_pick = jax.random.randint(key_pick, (domains, CELL_DEV, CELL_NODES), 0, 2 ** 30) % span_size
    left_bound = NODE_DEV + left_used[:, None, None]
    shifted = raw_pick - left_used[:, None, None] + GHOSTS
    local_index = jnp.where(raw_pick < left_bound, raw_pick, shifted)
    local_index = local_index.at[0, 0, 0].set(NODE_DEV + 2 * GHOSTS - 1).at[0, 0, 1].set(0)
    return local_index.reshape(CELLS, CELL_NODES).astype(jnp.int32)


def draw_send_lists(key, part):
    key = jax.random.fold_in(key, 7)
    domains = CELLS // CELL_DEV
    chosen = jax.random.randint(key, (domains, 2, GHOSTS), 0, NODE_DEV)
    chosen = chosen.at[1, 0, 0].set(0).at[1, 0, 1].set(NODE_DEV - 1)
    return chosen.astype(jnp.int32)


def shard_levels(key, dims, shards, low, largest):
    def one(dim, blocks):
        draws = jax.random.uniform(jax.random.fold_in(jax.random.fold_in(key, 6), dim), (blocks,), jnp.float32, low / len(shards), largest / len(shards))
        return jnp.repeat(jnp.exp(draws), dims[dim] // blocks).reshape((-1,) + (1,) * (len(dims) - dim - 1))

    level = one(*shards[0])
    for cut in shards[1:]:
        level = level * one(*cut)
    return level


def setup_inputs(seed: int = 0) -> dict:
    arg_keys = jax.random.split(jax.random.key(seed), 7)
    block = draw_block(jax.random.fold_in(arg_keys[6], 71), 0)
    cell_nodes = draw_cell_nodes(jax.random.fold_in(arg_keys[6], 71), 0)
    send_lists = draw_send_lists(jax.random.fold_in(arg_keys[6], 71), 0)
    cell_matrix = draw_cell_matrix(jax.random.fold_in(arg_keys[6], 71), 0)
    cell_scale = jnp.clip(jnp.exp(math.log(2.0) - 1.3862944 * jax.random.uniform(arg_keys[4], (CELLS,), jnp.float32) ** shard_levels(arg_keys[4], (CELLS,), ((0, 256),), -0.2, 0.2)), 0.5, 2.0)
    potential = jnp.clip(-1.0 + 1.5 * jax.random.uniform(arg_keys[5], (NODES,), jnp.float32) ** shard_levels(arg_keys[5], (NODES,), ((0, 256),), -0.2, 0.2), -1.0, 0.5)
    return dict(block=block, cell_nodes=cell_nodes, send_lists=send_lists, cell_matrix=cell_matrix, cell_scale=cell_scale, potential=potential)


def lower_solve(factor, right_hand):
    return lax.linalg.triangular_solve(factor, right_hand, left_side=True, lower=True)

def global_nodes(cell_nodes, send_lists):
    domains = CELLS // CELL_DEV
    owner_dom = (jnp.arange(CELLS, dtype=jnp.int32) // CELL_DEV)[:, None]
    left_dom = jnp.clip(owner_dom - 1, 0, domains - 1)
    right_dom = jnp.clip(owner_dom + 1, 0, domains - 1)
    left_slot = jnp.clip(cell_nodes - NODE_DEV, 0, GHOSTS - 1)
    right_slot = jnp.clip(cell_nodes - NODE_DEV - GHOSTS, 0, GHOSTS - 1)
    left_node = send_lists[left_dom, 1, left_slot]
    right_node = send_lists[right_dom, 0, right_slot]
    own_global = owner_dom * NODE_DEV + cell_nodes
    left_global = left_dom * NODE_DEV + left_node
    right_global = right_dom * NODE_DEV + right_node
    inner = jnp.where(cell_nodes < NODE_DEV + GHOSTS, left_global, right_global)
    return jnp.where(cell_nodes < NODE_DEV, own_global, inner).astype(jnp.int32)

def operate(states_in, global_index, cell_matrix, cell_scale, potential):
    domains = CELLS // CELL_DEV
    index_blocks = global_index.reshape(domains, CELL_DEV, CELL_NODES)
    scale_blocks = cell_scale.reshape(domains, CELL_DEV)
    matrix_wide = cell_matrix.astype(jnp.float32)

    def fold_cells(running, pieces):
        cell_index, cell_gain = pieces
        cell_grid = cell_index.T
        gathered = states_in[:, cell_grid].astype(jnp.float32)
        product = jnp.einsum('ij,sjc->sic', matrix_wide, gathered) * cell_gain[None, None, :]
        return (running.at[:, cell_grid].add(product), None)
    start = jnp.zeros(states_in.shape, jnp.float32)
    running, unused = lax.scan(fold_cells, start, (index_blocks, scale_blocks))
    return running + potential[None, :] * states_in.astype(jnp.float32)

def reference(block, cell_nodes, send_lists, cell_matrix, cell_scale, potential):
    global_index = global_nodes(cell_nodes, send_lists)
    filter_one = operate(block, global_index, cell_matrix, cell_scale, potential).astype(jnp.bfloat16)
    filter_two = (2.0 * operate(filter_one, global_index, cell_matrix, cell_scale, potential) - block.astype(jnp.float32)).astype(jnp.bfloat16)
    filtered = (2.0 * operate(filter_two, global_index, cell_matrix, cell_scale, potential) - filter_one.astype(jnp.float32)).astype(jnp.bfloat16)
    image = operate(filtered, global_index, cell_matrix, cell_scale, potential).astype(jnp.bfloat16)
    gram = jnp.dot(filtered.astype(jnp.float32), filtered.T.astype(jnp.float32), preferred_element_type=jnp.float32) / NODES
    hamiltonian = jnp.dot(filtered.astype(jnp.float32), image.T.astype(jnp.float32), preferred_element_type=jnp.float32) / NODES
    factor = jnp.linalg.cholesky(gram)
    ortho_block = lower_solve(factor, filtered.astype(jnp.float32))
    half_solved = lower_solve(factor, hamiltonian)
    projected = lower_solve(factor, half_solved.T).T
    return (ortho_block, projected)
```

```python
import jax
import jax.numpy as jnp
from jax import lax
from jax.experimental import pallas as pl
from jax.experimental.pallas import tpu as pltpu
from jax.sharding import PartitionSpec as P

BOTH = ("dom", "band")
BF16 = jnp.bfloat16
F32 = jnp.float32
CELL_PAD = 128
MIB = 1 << 20


def spec(space=pltpu.VMEM):
    return pl.BlockSpec(memory_space=space)


def nn(a, b):
    return lax.dot_general(a, b, (((1,), (0,)), ((), ())), preferred_element_type=F32)


def nt(a, b):
    return lax.dot_general(a, b, (((1,), (1,)), ((), ())), preferred_element_type=F32)


def one_hot(rows, row):
    hit = lax.broadcasted_iota(row.dtype, (rows, row.shape[1]), 0) == row
    return hit.astype(F32).astype(BF16)


def pair_mask(column, row):
    return (column == row).astype(F32).astype(BF16)


def send_body(block_ref, lists_ref, left_ref, right_ref):
    own = block_ref.shape[1]
    states = block_ref.shape[0]
    lists = lists_ref[...]
    slots = lists.shape[1]
    part = lax.broadcasted_iota(jnp.int32, (16, slots), 0)
    codes = jnp.zeros((16, slots), jnp.int32)
    for side in (0, 1):
        one = lists[side : side + 1]
        codes = jnp.where(part == 2 * side, one >> 5, codes)
        codes = jnp.where(part == 2 * side + 1, one & 31, codes)
    codes = codes.astype(F32).astype(BF16)
    for side, out in ((0, left_ref), (1, right_ref)):
        out[0:states, :] = nn(block_ref[...], one_hot(own, lists[side : side + 1])).astype(BF16)
        out[states : states + 16, :] = codes


def send_first(block, lists):
    states, slots = block.shape[0], lists.shape[1]
    shape = jax.ShapeDtypeStruct((states + 16, slots), BF16)
    return pl.pallas_call(
        send_body,
        out_shape=(shape, shape),
        in_specs=[spec()] * 2,
        out_specs=(spec(), spec()),
        name="send_first",
    )(block, lists)


def build_body(band_ref, nodes_ref, matrix_ref, scale_ref, out_ref, ids, mats, hot, left):
    cells, entries = nodes_ref.shape
    half, full = out_ref.shape
    ids[...] = jnp.full(ids.shape, -1, jnp.int32)
    ids[:, 0:entries] = nodes_ref[...]
    mats[...] = jnp.zeros(mats.shape, F32)
    matrix = matrix_ref[...].astype(F32)
    mats[0:entries, 0:entries] = matrix
    mats[CELL_PAD : CELL_PAD + entries, CELL_PAD : CELL_PAD + entries] = matrix
    pair_matrix = mats[...].astype(BF16)
    first = pl.multiple_of(band_ref[0] * half, 128)
    lane = lax.broadcasted_iota(jnp.int32, (1, 2 * CELL_PAD), 1)
    for pair in range(cells // 2):
        cols = slice(pair * 2 * CELL_PAD, (pair + 1) * 2 * CELL_PAD)
        for one in (0, 1):
            c = 2 * pair + one
            hot[:, c * CELL_PAD : (c + 1) * CELL_PAD] = one_hot(full, ids[c : c + 1, :])
        gain = jnp.where(lane < CELL_PAD, scale_ref[2 * pair], scale_ref[2 * pair + 1])
        left[:, cols] = (nt(hot[pl.ds(first, half), cols], pair_matrix) * gain).astype(BF16)

    @pl.loop(0, full // 256)
    def _(tile):
        rows = pl.ds(pl.multiple_of(tile * 256, 256), 256)
        out_ref[:, rows] = nt(left[...], hot[rows, :]).astype(BF16)


def build(band, cell_nodes, cell_matrix, cell_scale, full):
    cells = cell_nodes.shape[0]
    half = full // 2
    entries = cells * CELL_PAD
    return pl.pallas_call(
        build_body,
        out_shape=jax.ShapeDtypeStruct((half, full), BF16),
        in_specs=[spec(pltpu.SMEM), spec(), spec(), spec(pltpu.SMEM)],
        out_specs=spec(),
        scratch_shapes=[
            pltpu.VMEM((cells, CELL_PAD), jnp.int32),
            pltpu.VMEM((2 * CELL_PAD, 2 * CELL_PAD), F32),
            pltpu.VMEM((full, entries), BF16),
            pltpu.VMEM((half, entries), BF16),
        ],
        compiler_params=pltpu.CompilerParams(vmem_limit_bytes=44 * MIB),
        cost_estimate=pl.CostEstimate(
            flops=2 * half * entries * full, bytes_accessed=2 * half * full, transcendentals=0
        ),
        name="build",
    )(band, cell_nodes, cell_matrix, cell_scale)


def decode(codes_ref):
    slots = codes_ref.shape[1]
    codes = codes_ref[codes_ref.shape[0] - 16 :, :].astype(F32)
    rows = [codes[2 * s : 2 * s + 1] * 32.0 + codes[2 * s + 1 : 2 * s + 2] for s in (0, 1)]
    part = lax.broadcasted_iota(jnp.int32, (8, slots), 0)
    both = jnp.where(part == 0, rows[0], rows[1])
    columns = both.T
    return rows, [columns[:, 0:1], columns[:, 1:2]]


def assemble(partial_ref, ghost_ref, got_ref, lists, from_left_ref, from_right_ref, own):
    slots = lists.shape[1]
    (left_rows, left_cols), (right_rows, right_cols) = decode(from_left_ref), decode(from_right_ref)
    ghost = ghost_ref[...]
    ghost_left, ghost_right = ghost[:, 0:slots], ghost[:, slots : 2 * slots]
    states = ghost.shape[0]
    got_left, got_right = got_ref[0:states, :], got_ref[states : 2 * states, :]
    near_left, near_right = got_left[:, 0:slots], got_right[:, 0:slots]
    whole_own = (
        partial_ref[...]
        + nt(near_left, one_hot(own, lists[0:1]))
        + nt(near_right, one_hot(own, lists[1:2]))
    )
    whole_left = (
        got_left[:, slots : 2 * slots].astype(F32)
        + nn(got_left[:, 2 * slots : 3 * slots], pair_mask(left_cols[0], left_rows[1]))
        + nn(ghost_left, pair_mask(left_cols[1], left_rows[1]))
    )
    whole_right = (
        got_right[:, slots : 2 * slots].astype(F32)
        + nn(got_right[:, 2 * slots : 3 * slots], pair_mask(right_cols[1], right_rows[0]))
        + nn(ghost_right, pair_mask(right_cols[0], right_rows[0]))
    )
    return whole_own, whole_left, whole_right


def apply_body(band_ref, x, w_ref, potential_ref, lists, partial_out, ghost_out, near_out, far_out):
    own = partial_out.shape[1]
    slots = lists.shape[1]
    result = nn(x, w_ref[...])
    partial = result[:, 0:own] + potential_ref[...] * x[:, 0:own].astype(F32)
    partial_out[...] = partial
    ghost = result[:, own:].astype(BF16)
    ghost_out[...] = ghost
    right = band_ref[0] == 1
    mine = jnp.where(right, lists[1:2], lists[0:1])
    edge = jnp.where(right, ghost[:, slots : 2 * slots], ghost[:, 0:slots])
    near_out[:, 0:slots] = edge
    near_out[:, slots : 2 * slots] = nn(partial.astype(BF16), one_hot(own, mine)).astype(BF16)
    far_out[...] = edge


def first_body(band_ref, x_ref, w_ref, potential_ref, lists_ref, partial_out, ghost_out, near_out, far_out):
    apply_body(
        band_ref, x_ref[...], w_ref, potential_ref, lists_ref[...], partial_out, ghost_out, near_out, far_out
    )


def new_states(older_ref, x_out, pieces):
    own = pieces[0].shape[1]
    slots = pieces[1].shape[1]
    at = 0
    for piece in pieces:
        cols = slice(at, at + piece.shape[1])
        if older_ref is not None:
            piece = 2.0 * piece - older_ref[:, cols].astype(F32)
        x_out[:, cols] = piece.astype(BF16)
        at += piece.shape[1]


def next_body(chebyshev, *refs):
    if chebyshev:
        band_ref, w_ref, potential_ref, lists_ref, fl_ref, fr_ref, partial_ref, ghost_ref, got_ref, older_ref = refs[:10]
        refs = refs[10:]
    else:
        band_ref, w_ref, potential_ref, lists_ref, fl_ref, fr_ref, partial_ref, ghost_ref, got_ref = refs[:9]
        older_ref, refs = None, refs[9:]
    x_out, partial_out, ghost_out, near_out, far_out = refs
    lists = lists_ref[...]
    own = partial_ref.shape[1]
    new_states(older_ref, x_out, assemble(partial_ref, ghost_ref, got_ref, lists, fl_ref, fr_ref, own))
    apply_body(
        band_ref, x_out[...], w_ref, potential_ref, lists, partial_out, ghost_out, near_out, far_out
    )


def last_body(
    band_ref, w_ref, potential_ref, lists_ref, fl_ref, fr_ref, partial_ref, ghost_ref, got_ref, older_ref,
    own_out, sums_out, x_all, pot,
):
    lists = lists_ref[...]
    own = partial_ref.shape[1]
    states = partial_ref.shape[0]
    slots = lists.shape[1]
    new_states(older_ref, x_all, assemble(partial_ref, ghost_ref, got_ref, lists, fl_ref, fr_ref, own))
    pot[...] = potential_ref[...]
    half = own // 2
    mine = pl.ds(pl.multiple_of(band_ref[0] * half, 128), half)
    edge = pl.ds(pl.multiple_of(own + band_ref[0] * slots, 128), slots)
    x = x_all[...]
    x_mine = x_all[:, mine]
    own_out[...] = x_mine
    sums_out[:, 0:states] = nt(x_mine, x_mine)
    image = (nn(x, w_ref[:, mine]) + pot[:, mine] * x_mine.astype(F32)).astype(BF16)
    image_edge = nn(x, w_ref[:, edge]).astype(BF16)
    sums_out[:, states : 2 * states] = nt(x_mine, image) + nt(x_all[:, edge], image_edge)


def apply_shapes(states, own, slots):
    return (
        jax.ShapeDtypeStruct((states, own), F32),
        jax.ShapeDtypeStruct((states, 2 * slots), BF16),
        jax.ShapeDtypeStruct((states, 2 * slots), BF16),
        jax.ShapeDtypeStruct((states, slots), BF16),
    )


def stage_call(body, args, shapes, name, scratch=()):
    return pl.pallas_call(
        body,
        out_shape=tuple(shapes),
        in_specs=[spec(pltpu.SMEM)] + [spec()] * (len(args) - 1),
        out_specs=tuple(spec() for _ in shapes),
        scratch_shapes=list(scratch),
        compiler_params=pltpu.CompilerParams(vmem_limit_bytes=32 * MIB),
        name=name,
    )(*args)


def shift(x, axis, by):
    devices = lax.axis_size(axis)
    return lax.ppermute(x, axis, [(i, i + by) for i in range(devices) if 0 <= i + by < devices])


def across(x, by):
    parts = lax.axis_size("dom")
    pairs = [(2 * d + 1, 2 * (d + by)) for d in range(parts - by)]
    pairs += [(2 * (d + by), 2 * d + 1) for d in range(parts - by)]
    return lax.ppermute(x, BOTH, pairs)


def exchange(near, far):
    got = jnp.concatenate([across(near, 1), across(far, 2)], axis=1)
    return lax.all_gather(got, "band", axis=0, tiled=True)


def group_lists():
    eights, along_z, along_x = {}, {}, {}
    for x in range(4):
        for z in range(16):
            for y in range(4):
                for b in range(2):
                    i = ((x * 16 + z) * 4 + y) * 2 + b
                    eights.setdefault((x, z), []).append(i)
                    along_z.setdefault((x, z // 8, y, b), []).append(i)
                    along_x.setdefault((z % 8, y, b), []).append(i)
    return [list(g.values()) for g in (eights, along_z, along_x)]


def swap_pieces(x, groups):
    return lax.all_to_all(x, BOTH, 0, 0, axis_index_groups=groups, tiled=True)


def sum_everywhere(x):
    rows, cols = x.shape
    eights, along_z, along_x = group_lists()
    piece = swap_pieces(x, eights).reshape(8, rows // 8, cols).sum(0)
    for groups in (along_z, along_x):
        copies = jnp.broadcast_to(piece[None], (8,) + piece.shape).reshape(rows, cols)
        piece = swap_pieces(copies, groups).reshape(8, rows // 8, cols).sum(0)
    copies = jnp.broadcast_to(piece[None], (8,) + piece.shape).reshape(rows, cols)
    return swap_pieces(copies, eights)


def lower_solve(factor, right_hand):
    return lax.linalg.triangular_solve(factor, right_hand, left_side=True, lower=True)


def shards(block, cell_nodes, send_lists, cell_matrix, cell_scale, potential):
    lists = send_lists[0]
    own, slots = block.shape[1], lists.shape[1]
    full = own + 2 * slots
    states_here = block.shape[0]
    states = 2 * states_here
    band = lax.axis_index("band").astype(jnp.int32).reshape(1)
    potential = potential.reshape(1, own)

    to_left, to_right = send_first(block, lists)
    from_left = shift(to_right, "dom", 1)
    from_right = shift(to_left, "dom", -1)
    mine = build(band, cell_nodes, cell_matrix, cell_scale, full)
    other = lax.ppermute(mine, "band", [(0, 1), (1, 0)])
    first = band[0] == 0
    w = jnp.concatenate([jnp.where(first, mine, other), jnp.where(first, other, mine)], axis=0)
    x_here = jnp.concatenate([block, from_left[:states_here], from_right[:states_here]], axis=1)
    x0 = lax.all_gather(x_here, "band", axis=0, tiled=True)

    shapes = apply_shapes(states, own, slots)
    x_shape = jax.ShapeDtypeStruct((states, full), BF16)
    fixed = (band, w, potential, lists, from_left, from_right)
    partial, ghost, near, far = stage_call(first_body, (band, x0, w, potential, lists), shapes, "apply_one")
    got = exchange(near, far)
    x1, partial, ghost, near, far = stage_call(
        lambda *r: next_body(False, *r), fixed + (partial, ghost, got), (x_shape,) + shapes, "apply_two"
    )
    got = exchange(near, far)
    x2, partial, ghost, near, far = stage_call(
        lambda *r: next_body(True, *r), fixed + (partial, ghost, got, x0), (x_shape,) + shapes, "apply_three"
    )
    got = exchange(near, far)
    own_part, sums = stage_call(
        last_body,
        fixed + (partial, ghost, got, x1),
        (jax.ShapeDtypeStruct((states, own // 2), BF16), jax.ShapeDtypeStruct((states, 2 * states), F32)),
        "apply_four",
        (pltpu.VMEM((states, full), BF16), pltpu.VMEM((1, own), F32)),
    )
    total = sum_everywhere(sums) / (own * lax.axis_size("dom"))
    gram, hamiltonian = total[:, :states], total[:, states:]
    factor = jnp.linalg.cholesky(gram)
    ortho_block = lower_solve(factor, own_part.astype(F32))
    half_solved = lower_solve(factor, hamiltonian)
    projected = lower_solve(factor, half_solved.T).T
    return (ortho_block, projected)


def solution(mesh):
    return jax.shard_map(
        shards,
        mesh=mesh,
        in_specs=(P("band", "dom"), P("dom", None), P("dom", None, None), P(), P("dom"), P("dom")),
        out_specs=(P(None, ("dom", "band")), P()),
        check_vma=False,
    )
```

```python
import jax
import jax.numpy as jnp
from jax import lax
from jax.experimental import pallas as pl
from jax.experimental.pallas import tpu as pltpu
from jax.sharding import PartitionSpec as P

BOTH = ("dom", "band")
BF16 = jnp.bfloat16
F32 = jnp.float32
CELL_PAD = 128
MIB = 1 << 20


def spec(space=pltpu.VMEM):
    return pl.BlockSpec(memory_space=space)


def nn(a, b):
    return lax.dot_general(a, b, (((1,), (0,)), ((), ())), preferred_element_type=F32)


def nt(a, b):
    return lax.dot_general(a, b, (((1,), (1,)), ((), ())), preferred_element_type=F32)


def one_hot(rows, row):
    hit = lax.broadcasted_iota(row.dtype, (rows, row.shape[1]), 0) == row
    return hit.astype(F32).astype(BF16)


def pair_mask(column, row):
    return (column == row).astype(F32).astype(BF16)


def send_body(block_ref, lists_ref, left_ref, right_ref):
    own = block_ref.shape[1]
    states = block_ref.shape[0]
    lists = lists_ref[...]
    slots = lists.shape[1]
    part = lax.broadcasted_iota(jnp.int32, (16, slots), 0)
    codes = jnp.zeros((16, slots), jnp.int32)
    for side in (0, 1):
        one = lists[side : side + 1]
        codes = jnp.where(part == 2 * side, one >> 5, codes)
        codes = jnp.where(part == 2 * side + 1, one & 31, codes)
    codes = codes.astype(F32).astype(BF16)
    for side, out in ((0, left_ref), (1, right_ref)):
        out[0:states, :] = nn(block_ref[...], one_hot(own, lists[side : side + 1])).astype(BF16)
        out[states : states + 16, :] = codes


def send_first(block, lists):
    states, slots = block.shape[0], lists.shape[1]
    shape = jax.ShapeDtypeStruct((states + 16, slots), BF16)
    return pl.pallas_call(
        send_body,
        out_shape=(shape, shape),
        in_specs=[spec()] * 2,
        out_specs=(spec(), spec()),
        name="send_first",
    )(block, lists)


def build_body(band_ref, nodes_ref, matrix_ref, scale_ref, out_ref, ids, mats, hot, left):
    cells, entries = nodes_ref.shape
    half, full = out_ref.shape
    ids[...] = jnp.full(ids.shape, -1, jnp.int32)
    ids[:, 0:entries] = nodes_ref[...]
    mats[...] = jnp.zeros(mats.shape, F32)
    matrix = matrix_ref[...].astype(F32)
    mats[0:entries, 0:entries] = matrix
    mats[CELL_PAD : CELL_PAD + entries, CELL_PAD : CELL_PAD + entries] = matrix
    pair_matrix = mats[...].astype(BF16)
    first = pl.multiple_of(band_ref[0] * half, 128)
    lane = lax.broadcasted_iota(jnp.int32, (1, 2 * CELL_PAD), 1)
    for pair in range(cells // 2):
        cols = slice(pair * 2 * CELL_PAD, (pair + 1) * 2 * CELL_PAD)
        for one in (0, 1):
            c = 2 * pair + one
            hot[:, c * CELL_PAD : (c + 1) * CELL_PAD] = one_hot(full, ids[c : c + 1, :])
        gain = jnp.where(lane < CELL_PAD, scale_ref[2 * pair], scale_ref[2 * pair + 1])
        left[:, cols] = (nt(hot[pl.ds(first, half), cols], pair_matrix) * gain).astype(BF16)

    @pl.loop(0, full // 256)
    def _(tile):
        rows = pl.ds(pl.multiple_of(tile * 256, 256), 256)
        out_ref[:, rows] = nt(left[...], hot[rows, :]).astype(BF16)


def build(band, cell_nodes, cell_matrix, cell_scale, full):
    cells = cell_nodes.shape[0]
    half = full // 2
    entries = cells * CELL_PAD
    return pl.pallas_call(
        build_body,
        out_shape=jax.ShapeDtypeStruct((half, full), BF16),
        in_specs=[spec(pltpu.SMEM), spec(), spec(), spec(pltpu.SMEM)],
        out_specs=spec(),
        scratch_shapes=[
            pltpu.VMEM((cells, CELL_PAD), jnp.int32),
            pltpu.VMEM((2 * CELL_PAD, 2 * CELL_PAD), F32),
            pltpu.VMEM((full, entries), BF16),
            pltpu.VMEM((half, entries), BF16),
        ],
        compiler_params=pltpu.CompilerParams(vmem_limit_bytes=44 * MIB),
        cost_estimate=pl.CostEstimate(
            flops=2 * half * entries * full, bytes_accessed=2 * half * full, transcendentals=0
        ),
        name="build",
    )(band, cell_nodes, cell_matrix, cell_scale)


def decode(codes_ref):
    slots = codes_ref.shape[1]
    codes = codes_ref[codes_ref.shape[0] - 16 :, :].astype(F32)
    rows = [codes[2 * s : 2 * s + 1] * 32.0 + codes[2 * s + 1 : 2 * s + 2] for s in (0, 1)]
    part = lax.broadcasted_iota(jnp.int32, (8, slots), 0)
    both = jnp.where(part == 0, rows[0], rows[1])
    columns = both.T
    return rows, [columns[:, 0:1], columns[:, 1:2]]


def assemble(partial_ref, ghost_ref, got_ref, lists, from_left_ref, from_right_ref, own):
    slots = lists.shape[1]
    (left_rows, left_cols), (right_rows, right_cols) = decode(from_left_ref), decode(from_right_ref)
    ghost = ghost_ref[...]
    ghost_left, ghost_right = ghost[:, 0:slots], ghost[:, slots : 2 * slots]
    states = ghost.shape[0]
    got_left, got_right = got_ref[0:states, :], got_ref[states : 2 * states, :]
    near_left, near_right = got_left[:, 0:slots], got_right[:, 0:slots]
    whole_own = (
        partial_ref[...]
        + nt(near_left, one_hot(own, lists[0:1]))
        + nt(near_right, one_hot(own, lists[1:2]))
    )
    whole_left = (
        got_left[:, slots : 2 * slots].astype(F32)
        + nn(got_left[:, 2 * slots : 3 * slots], pair_mask(left_cols[0], left_rows[1]))
        + nn(ghost_left, pair_mask(left_cols[1], left_rows[1]))
    )
    whole_right = (
        got_right[:, slots : 2 * slots].astype(F32)
        + nn(got_right[:, 2 * slots : 3 * slots], pair_mask(right_cols[1], right_rows[0]))
        + nn(ghost_right, pair_mask(right_cols[0], right_rows[0]))
    )
    return whole_own, whole_left, whole_right


def times_operator(band, x_ref, mine_ref, other_ref, cols):
    half = mine_ref.shape[0]
    here = pl.ds(pl.multiple_of(band * half, 128), half)
    there = pl.ds(pl.multiple_of((1 - band) * half, 128), half)
    return nn(x_ref[:, here], mine_ref[:, cols]) + nn(x_ref[:, there], other_ref[:, cols])


def apply_body(
    band_ref, x_ref, mine_ref, other_ref, potential_ref, lists, partial_out, ghost_out, near_out, far_out
):
    own = partial_out.shape[1]
    slots = lists.shape[1]
    result = times_operator(band_ref[0], x_ref, mine_ref, other_ref, slice(None))
    partial = result[:, 0:own] + potential_ref[...] * x_ref[:, 0:own].astype(F32)
    partial_out[...] = partial
    ghost = result[:, own:].astype(BF16)
    ghost_out[...] = ghost
    right = band_ref[0] == 1
    mine = jnp.where(right, lists[1:2], lists[0:1])
    edge = jnp.where(right, ghost[:, slots : 2 * slots], ghost[:, 0:slots])
    near_out[:, 0:slots] = edge
    near_out[:, slots : 2 * slots] = nn(partial.astype(BF16), one_hot(own, mine)).astype(BF16)
    far_out[...] = edge


def first_body(band_ref, mine_ref, other_ref, potential_ref, lists_ref, x_ref, *outs):
    apply_body(band_ref, x_ref, mine_ref, other_ref, potential_ref, lists_ref[...], *outs)


def new_states(older_ref, x_out, pieces):
    own = pieces[0].shape[1]
    slots = pieces[1].shape[1]
    at = 0
    for piece in pieces:
        cols = slice(at, at + piece.shape[1])
        if older_ref is not None:
            piece = 2.0 * piece - older_ref[:, cols].astype(F32)
        x_out[:, cols] = piece.astype(BF16)
        at += piece.shape[1]


def next_body(chebyshev, *refs):
    band_ref, mine_ref, other_ref, potential_ref, lists_ref, fl_ref, fr_ref, partial_ref, ghost_ref, got_ref = refs[:10]
    older_ref = refs[10] if chebyshev else None
    x_out, *outs = refs[11:] if chebyshev else refs[10:]
    lists = lists_ref[...]
    own = partial_ref.shape[1]
    new_states(older_ref, x_out, assemble(partial_ref, ghost_ref, got_ref, lists, fl_ref, fr_ref, own))
    apply_body(band_ref, x_out, mine_ref, other_ref, potential_ref, lists, *outs)


def last_body(
    band_ref, mine_ref, other_ref, potential_ref, lists_ref, fl_ref, fr_ref, partial_ref, ghost_ref, got_ref,
    older_ref, own_out, sums_out, x_all, pot,
):
    lists = lists_ref[...]
    own = partial_ref.shape[1]
    states = partial_ref.shape[0]
    slots = lists.shape[1]
    new_states(older_ref, x_all, assemble(partial_ref, ghost_ref, got_ref, lists, fl_ref, fr_ref, own))
    pot[...] = potential_ref[...]
    half = own // 2
    mine = pl.ds(pl.multiple_of(band_ref[0] * half, 128), half)
    edge = pl.ds(pl.multiple_of(own + band_ref[0] * slots, 128), slots)
    x_mine = x_all[:, mine]
    own_out[...] = x_mine
    sums_out[0:states, :] = nt(x_mine, x_mine)
    image = times_operator(band_ref[0], x_all, mine_ref, other_ref, mine) + pot[:, mine] * x_mine.astype(F32)
    image_edge = times_operator(band_ref[0], x_all, mine_ref, other_ref, edge)
    sums_out[states : 2 * states, :] = nt(x_mine, image.astype(BF16)) + nt(x_all[:, edge], image_edge.astype(BF16))


def apply_shapes(states, own, slots):
    return (
        jax.ShapeDtypeStruct((states, own), F32),
        jax.ShapeDtypeStruct((states, 2 * slots), BF16),
        jax.ShapeDtypeStruct((states, 2 * slots), BF16),
        jax.ShapeDtypeStruct((states, slots), BF16),
    )


def stage_call(body, args, shapes, name, scratch=()):
    return pl.pallas_call(
        body,
        out_shape=tuple(shapes),
        in_specs=[spec(pltpu.SMEM)] + [spec()] * (len(args) - 1),
        out_specs=tuple(spec() for _ in shapes),
        scratch_shapes=list(scratch),
        compiler_params=pltpu.CompilerParams(vmem_limit_bytes=32 * MIB),
        name=name,
    )(*args)


def shift(x, axis, by):
    devices = lax.axis_size(axis)
    return lax.ppermute(x, axis, [(i, i + by) for i in range(devices) if 0 <= i + by < devices])


def across(x, by):
    parts = lax.axis_size("dom")
    pairs = [(2 * d + 1, 2 * (d + by)) for d in range(parts - by)]
    pairs += [(2 * (d + by), 2 * d + 1) for d in range(parts - by)]
    return lax.ppermute(x, BOTH, pairs)


def exchange(near, far):
    got = jnp.concatenate([across(near, 1), across(far, 2)], axis=1)
    return lax.all_gather(got, "band", axis=0, tiled=True)


def group_lists():
    planes, along_z = {}, {}
    for x in range(4):
        for z in range(16):
            for y in range(4):
                for b in range(2):
                    i = ((x * 16 + z) * 4 + y) * 2 + b
                    planes.setdefault(z, []).append(i)
                    along_z.setdefault((x, y, b), []).append(i)
    return list(planes.values()), list(along_z.values())


def swap_pieces(x, groups):
    return lax.all_to_all(x, BOTH, 0, 0, axis_index_groups=groups, tiled=True)


def copies(piece, count):
    return jnp.broadcast_to(piece[None], (count,) + piece.shape).reshape(count * piece.shape[0], piece.shape[1])


def sum_pieces(x, count):
    return x.reshape(count, x.shape[0] // count, x.shape[1]).sum(0)


def sum_everywhere(x):
    planes, along_z = group_lists()
    in_plane, depth = len(planes[0]), len(along_z[0])
    piece = sum_pieces(swap_pieces(x, planes), in_plane)
    piece = sum_pieces(swap_pieces(copies(piece, depth), along_z), depth)
    return swap_pieces(copies(piece, in_plane), planes)


def exact(a, b):
    return jnp.dot(a, b, precision=lax.Precision.HIGHEST, preferred_element_type=F32)


def weighted(weights, rows):
    total = None
    for w, r in zip(weights, rows):
        total = w * r if total is None else total + w * r
    return total


def stack(rows):
    part = lax.broadcasted_iota(jnp.int32, rows[0].shape, 0)
    out = rows[0]
    for i in range(1, len(rows)):
        out = jnp.where(part == i, rows[i], out)
    return out


def inverse_of_eight(panel, first):
    wide = panel.shape
    columns = [jnp.broadcast_to(panel[:, first + j : first + j + 1], wide) for j in range(8)]
    low = {(i, j): jnp.broadcast_to(columns[j][i : i + 1, :], wide) for j in range(8) for i in range(j, 8)}
    inv = {}
    for j in range(8):
        inv[j, j] = lax.rsqrt(low[j, j])
        for i in range(j + 1, 8):
            low[i, j] = low[i, j] * inv[j, j]
        for k in range(j + 1, 8):
            for i in range(k, 8):
                low[i, k] = low[i, k] - low[i, j] * low[k, j]
        for k in range(j):
            inv[j, k] = -inv[j, j] * weighted([low[j, m] for m in range(k, j)], [inv[m, k] for m in range(k, j)])
    return inv


def finish_body(scale, total_ref, own_ref, ortho_out, projected_out, inverse_ref):
    size = total_ref.shape[1]
    schur = total_ref[0:size, :] * scale
    at = lax.broadcasted_iota(jnp.int32, (size, size), 0)
    beside = (at == lax.broadcasted_iota(jnp.int32, (size, size), 1)).astype(F32)
    for first in range(0, size, 8):
        top, top_beside = schur[0:8], beside[0:8]
        inv = inverse_of_eight(top, first)
        rows = [jnp.broadcast_to(top[i : i + 1], top.shape) for i in range(8)]
        rows_beside = [jnp.broadcast_to(top_beside[i : i + 1], top.shape) for i in range(8)]
        solved = [weighted([inv[i, k] for k in range(i + 1)], rows) for i in range(8)]
        solved_beside = [weighted([inv[i, k] for k in range(i + 1)], rows_beside) for i in range(8)]
        inverse_ref[first : first + 8, :] = stack(solved_beside)
        if first + 8 == size:
            break
        twice = stack([weighted([inv[k, i] for k in range(i, 8)], solved[i:]) for i in range(8)])
        twice_beside = stack([weighted([inv[k, i] for k in range(i, 8)], solved_beside[i:]) for i in range(8)])
        both = jnp.concatenate([twice, twice_beside], axis=1)
        pieces = [both]
        if first:
            pieces = [jnp.zeros((first, 2 * size), F32)] + pieces
        pieces.append(jnp.zeros((size - first - 8, 2 * size), F32))
        taken = exact(schur[8:], jnp.concatenate(pieces, axis=0))
        schur = schur[8:] - taken[:, 0:size]
        beside = beside[8:] - taken[:, size:]
    inverse = inverse_ref[...]
    coarse = inverse.astype(BF16)
    rest = inverse - coarse.astype(F32)
    fine = rest.astype(BF16)
    finest = (rest - fine.astype(F32)).astype(BF16)
    own = own_ref[...]
    ortho_out[...] = nn(coarse, own) + (nn(fine, own) + nn(finest, own))
    half_solved = exact(inverse, total_ref[size : 2 * size, :] * scale)
    projected_out[...] = lax.dot_general(
        half_solved, inverse, (((1,), (1,)), ((), ())), precision=lax.Precision.HIGHEST, preferred_element_type=F32
    )


def finish(scale, total, own_part):
    states, nodes = own_part.shape
    return pl.pallas_call(
        lambda *refs: finish_body(scale, *refs),
        out_shape=(jax.ShapeDtypeStruct((states, nodes), F32), jax.ShapeDtypeStruct((states, states), F32)),
        in_specs=[spec()] * 2,
        out_specs=(spec(), spec()),
        scratch_shapes=[pltpu.VMEM((states, states), F32)],
        compiler_params=pltpu.CompilerParams(vmem_limit_bytes=32 * MIB),
        name="finish",
    )(total, own_part)


def shards(block, cell_nodes, send_lists, cell_matrix, cell_scale, potential):
    lists = send_lists[0]
    own, slots = block.shape[1], lists.shape[1]
    full = own + 2 * slots
    states_here = block.shape[0]
    states = 2 * states_here
    band = lax.axis_index("band").astype(jnp.int32).reshape(1)
    potential = potential.reshape(1, own)

    to_left, to_right = send_first(block, lists)
    to_left, to_right, cell_nodes = lax.optimization_barrier((to_left, to_right, cell_nodes))
    from_left = shift(to_right, "dom", 1)
    from_right = shift(to_left, "dom", -1)
    mine = build(band, cell_nodes, cell_matrix, cell_scale, full)
    other = lax.ppermute(mine, "band", [(0, 1), (1, 0)])
    x_here = jnp.concatenate([block, from_left[:states_here], from_right[:states_here]], axis=1)
    x0 = lax.all_gather(x_here, "band", axis=0, tiled=True)

    shapes = apply_shapes(states, own, slots)
    x_shape = jax.ShapeDtypeStruct((states, full), BF16)
    fixed = (band, mine, other, potential, lists)
    ends = fixed + (from_left, from_right)
    partial, ghost, near, far = stage_call(first_body, fixed + (x0,), shapes, "apply_one")
    got = exchange(near, far)
    x1, partial, ghost, near, far = stage_call(
        lambda *r: next_body(False, *r), ends + (partial, ghost, got), (x_shape,) + shapes, "apply_two"
    )
    got = exchange(near, far)
    x2, partial, ghost, near, far = stage_call(
        lambda *r: next_body(True, *r), ends + (partial, ghost, got, x0), (x_shape,) + shapes, "apply_three"
    )
    got = exchange(near, far)
    own_part, sums = stage_call(
        last_body,
        ends + (partial, ghost, got, x1),
        (jax.ShapeDtypeStruct((states, own // 2), BF16), jax.ShapeDtypeStruct((2 * states, states), F32)),
        "apply_four",
        (pltpu.VMEM((states, full), BF16), pltpu.VMEM((1, own), F32)),
    )
    return finish(1.0 / (own * lax.axis_size("dom")), sum_everywhere(sums), own_part)


def solution(mesh):
    return jax.shard_map(
        shards,
        mesh=mesh,
        in_specs=(P("band", "dom"), P("dom", None), P("dom", None, None), P(), P("dom"), P("dom")),
        out_specs=(P(None, ("dom", "band")), P()),
        check_vma=False,
    )
```

```python
import jax
import jax.numpy as jnp
from jax import lax
from jax.experimental import pallas as pl
from jax.experimental.pallas import tpu as pltpu
from jax.sharding import PartitionSpec as P

BOTH = ("dom", "band")
BF16 = jnp.bfloat16
F32 = jnp.float32
CELL_PAD = 128
MIB = 1 << 20


def spec(space=pltpu.VMEM):
    return pl.BlockSpec(memory_space=space)


def nn(a, b):
    return lax.dot_general(a, b, (((1,), (0,)), ((), ())), preferred_element_type=F32)


def nt(a, b):
    return lax.dot_general(a, b, (((1,), (1,)), ((), ())), preferred_element_type=F32)


def one_hot(rows, row):
    hit = lax.broadcasted_iota(row.dtype, (rows, row.shape[1]), 0) == row
    return hit.astype(F32).astype(BF16)


def pair_mask(column, row):
    return (column == row).astype(F32).astype(BF16)


def send_body(block_ref, lists_ref, left_ref, right_ref):
    own = block_ref.shape[1]
    states = block_ref.shape[0]
    lists = lists_ref[...]
    slots = lists.shape[1]
    part = lax.broadcasted_iota(jnp.int32, (16, slots), 0)
    codes = jnp.zeros((16, slots), jnp.int32)
    for side in (0, 1):
        one = lists[side : side + 1]
        codes = jnp.where(part == 2 * side, one >> 5, codes)
        codes = jnp.where(part == 2 * side + 1, one & 31, codes)
    codes = codes.astype(F32).astype(BF16)
    for side, out in ((0, left_ref), (1, right_ref)):
        out[0:states, :] = nn(block_ref[...], one_hot(own, lists[side : side + 1])).astype(BF16)
        out[states : states + 16, :] = codes


def send_first(block, lists):
    states, slots = block.shape[0], lists.shape[1]
    shape = jax.ShapeDtypeStruct((states + 16, slots), BF16)
    return pl.pallas_call(
        send_body,
        out_shape=(shape, shape),
        in_specs=[spec()] * 2,
        out_specs=(spec(), spec()),
        name="send_first",
    )(block, lists)


def build_body(band_ref, nodes_ref, matrix_ref, scale_ref, out_ref, ids, mats, hot, left):
    cells, entries = nodes_ref.shape
    half, full = out_ref.shape
    ids[...] = jnp.full(ids.shape, -1, jnp.int32)
    ids[:, 0:entries] = nodes_ref[...]
    mats[...] = jnp.zeros(mats.shape, F32)
    matrix = matrix_ref[...].astype(F32)
    mats[0:entries, 0:entries] = matrix
    mats[CELL_PAD : CELL_PAD + entries, CELL_PAD : CELL_PAD + entries] = matrix
    pair_matrix = mats[...].T.astype(BF16)
    first = band_ref[0] * half
    lane = lax.broadcasted_iota(jnp.int32, (1, 2 * CELL_PAD), 1)
    for pair in range(cells // 2):
        rows = [ids[c : c + 1, :] for c in (2 * pair, 2 * pair + 1)]
        row = jnp.concatenate(rows, axis=1)
        cols = slice(pair * 2 * CELL_PAD, (pair + 1) * 2 * CELL_PAD)
        gain = jnp.where(lane < CELL_PAD, scale_ref[2 * pair], scale_ref[2 * pair + 1])
        left[:, cols] = (nn(one_hot(half, row - first), pair_matrix) * gain).astype(BF16)
        hot[:, cols] = one_hot(full, row)
    for at in range(0, half, 256):
        out_ref[at : at + 256, :] = nt(left[at : at + 256, :], hot[...]).astype(BF16)


def build(band, cell_nodes, cell_matrix, cell_scale, full):
    cells = cell_nodes.shape[0]
    half = full // 2
    entries = cells * CELL_PAD
    return pl.pallas_call(
        build_body,
        out_shape=jax.ShapeDtypeStruct((half, full), BF16),
        in_specs=[spec(pltpu.SMEM), spec(), spec(), spec(pltpu.SMEM)],
        out_specs=spec(),
        scratch_shapes=[
            pltpu.VMEM((cells, CELL_PAD), jnp.int32),
            pltpu.VMEM((2 * CELL_PAD, 2 * CELL_PAD), F32),
            pltpu.VMEM((full, entries), BF16),
            pltpu.VMEM((half, entries), BF16),
        ],
        compiler_params=pltpu.CompilerParams(vmem_limit_bytes=44 * MIB),
        cost_estimate=pl.CostEstimate(
            flops=2 * half * entries * full, bytes_accessed=2 * half * full, transcendentals=0
        ),
        name="build",
    )(band, cell_nodes, cell_matrix, cell_scale)


def decode(codes_ref):
    slots = codes_ref.shape[1]
    codes = codes_ref[codes_ref.shape[0] - 16 :, :].astype(F32)
    rows = [codes[2 * s : 2 * s + 1] * 32.0 + codes[2 * s + 1 : 2 * s + 2] for s in (0, 1)]
    part = lax.broadcasted_iota(jnp.int32, (8, slots), 0)
    both = jnp.where(part == 0, rows[0], rows[1])
    columns = both.T
    return rows, [columns[:, 0:1], columns[:, 1:2]]


def assemble(partial_ref, ghost_ref, got_ref, lists, from_left_ref, from_right_ref, own):
    slots = lists.shape[1]
    (left_rows, left_cols), (right_rows, right_cols) = decode(from_left_ref), decode(from_right_ref)
    ghost = ghost_ref[...]
    ghost_left, ghost_right = ghost[:, 0:slots], ghost[:, slots : 2 * slots]
    states = ghost.shape[0]
    got_left, got_right = got_ref[0:states, :], got_ref[states : 2 * states, :]
    near_left, near_right = got_left[:, 0:slots], got_right[:, 0:slots]
    whole_own = (
        partial_ref[...]
        + nt(near_left, one_hot(own, lists[0:1]))
        + nt(near_right, one_hot(own, lists[1:2]))
    )
    whole_left = (
        got_left[:, slots : 2 * slots].astype(F32)
        + nn(got_left[:, 2 * slots : 3 * slots], pair_mask(left_cols[0], left_rows[1]))
        + nn(ghost_left, pair_mask(left_cols[1], left_rows[1]))
    )
    whole_right = (
        got_right[:, slots : 2 * slots].astype(F32)
        + nn(got_right[:, 2 * slots : 3 * slots], pair_mask(right_cols[1], right_rows[0]))
        + nn(ghost_right, pair_mask(right_cols[0], right_rows[0]))
    )
    return whole_own, whole_left, whole_right


def times_operator(band, x_ref, mine_ref, other_ref, cols):
    half = mine_ref.shape[0]
    here = pl.ds(pl.multiple_of(band * half, 128), half)
    there = pl.ds(pl.multiple_of((1 - band) * half, 128), half)
    return nn(x_ref[:, here], mine_ref[:, cols]) + nn(x_ref[:, there], other_ref[:, cols])


def apply_body(
    band_ref, x_ref, mine_ref, other_ref, potential_ref, lists, partial_out, ghost_out, near_out, far_out
):
    own = partial_out.shape[1]
    slots = lists.shape[1]
    result = times_operator(band_ref[0], x_ref, mine_ref, other_ref, slice(None))
    partial = result[:, 0:own] + potential_ref[...] * x_ref[:, 0:own].astype(F32)
    partial_out[...] = partial
    ghost = result[:, own:].astype(BF16)
    ghost_out[...] = ghost
    right = band_ref[0] == 1
    mine = jnp.where(right, lists[1:2], lists[0:1])
    edge = jnp.where(right, ghost[:, slots : 2 * slots], ghost[:, 0:slots])
    near_out[:, 0:slots] = edge
    near_out[:, slots : 2 * slots] = nn(partial.astype(BF16), one_hot(own, mine)).astype(BF16)
    far_out[...] = edge


def first_body(band_ref, mine_ref, other_ref, potential_ref, lists_ref, x_ref, *outs):
    apply_body(band_ref, x_ref, mine_ref, other_ref, potential_ref, lists_ref[...], *outs)


def new_states(older_ref, x_out, pieces):
    own = pieces[0].shape[1]
    slots = pieces[1].shape[1]
    at = 0
    for piece in pieces:
        cols = slice(at, at + piece.shape[1])
        if older_ref is not None:
            piece = 2.0 * piece - older_ref[:, cols].astype(F32)
        x_out[:, cols] = piece.astype(BF16)
        at += piece.shape[1]


def next_body(chebyshev, *refs):
    band_ref, mine_ref, other_ref, potential_ref, lists_ref, fl_ref, fr_ref, partial_ref, ghost_ref, got_ref = refs[:10]
    older_ref = refs[10] if chebyshev else None
    x_out, *outs = refs[11:] if chebyshev else refs[10:]
    lists = lists_ref[...]
    own = partial_ref.shape[1]
    new_states(older_ref, x_out, assemble(partial_ref, ghost_ref, got_ref, lists, fl_ref, fr_ref, own))
    apply_body(band_ref, x_out, mine_ref, other_ref, potential_ref, lists, *outs)


def last_body(
    band_ref, mine_ref, other_ref, potential_ref, lists_ref, fl_ref, fr_ref, partial_ref, ghost_ref, got_ref,
    older_ref, own_out, sums_out, x_all, pot,
):
    lists = lists_ref[...]
    own = partial_ref.shape[1]
    states = partial_ref.shape[0]
    slots = lists.shape[1]
    new_states(older_ref, x_all, assemble(partial_ref, ghost_ref, got_ref, lists, fl_ref, fr_ref, own))
    pot[...] = potential_ref[...]
    half = own // 2
    mine = pl.ds(pl.multiple_of(band_ref[0] * half, 128), half)
    edge = pl.ds(pl.multiple_of(own + band_ref[0] * slots, 128), slots)
    x_mine = x_all[:, mine]
    own_out[...] = x_mine
    sums_out[0:states, :] = nt(x_mine, x_mine)
    image = times_operator(band_ref[0], x_all, mine_ref, other_ref, mine) + pot[:, mine] * x_mine.astype(F32)
    image_edge = times_operator(band_ref[0], x_all, mine_ref, other_ref, edge)
    sums_out[states : 2 * states, :] = nt(x_mine, image.astype(BF16)) + nt(x_all[:, edge], image_edge.astype(BF16))


def apply_shapes(states, own, slots):
    return (
        jax.ShapeDtypeStruct((states, own), F32),
        jax.ShapeDtypeStruct((states, 2 * slots), BF16),
        jax.ShapeDtypeStruct((states, 2 * slots), BF16),
        jax.ShapeDtypeStruct((states, slots), BF16),
    )


def stage_call(body, args, shapes, name, scratch=()):
    return pl.pallas_call(
        body,
        out_shape=tuple(shapes),
        in_specs=[spec(pltpu.SMEM)] + [spec()] * (len(args) - 1),
        out_specs=tuple(spec() for _ in shapes),
        scratch_shapes=list(scratch),
        compiler_params=pltpu.CompilerParams(vmem_limit_bytes=32 * MIB),
        name=name,
    )(*args)


def shift(x, axis, by):
    devices = lax.axis_size(axis)
    return lax.ppermute(x, axis, [(i, i + by) for i in range(devices) if 0 <= i + by < devices])


def across(x, by):
    parts = lax.axis_size("dom")
    pairs = [(2 * d + 1, 2 * (d + by)) for d in range(parts - by)]
    pairs += [(2 * (d + by), 2 * d + 1) for d in range(parts - by)]
    return lax.ppermute(x, BOTH, pairs)


def exchange(near, far):
    got = jnp.concatenate([across(near, 1), across(far, 2)], axis=1)
    return lax.all_gather(got, "band", axis=0, tiled=True)


def group_lists():
    planes, along_z = {}, {}
    for x in range(4):
        for z in range(16):
            for y in range(4):
                for b in range(2):
                    i = ((x * 16 + z) * 4 + y) * 2 + b
                    planes.setdefault(z, []).append(i)
                    along_z.setdefault((x, y, b), []).append(i)
    return list(planes.values()), list(along_z.values())


def swap_pieces(x, groups):
    return lax.all_to_all(x, BOTH, 0, 0, axis_index_groups=groups, tiled=True)


def copies(piece, count):
    return jnp.broadcast_to(piece[None], (count,) + piece.shape).reshape(count * piece.shape[0], piece.shape[1])


def sum_pieces(x, count):
    return x.reshape(count, x.shape[0] // count, x.shape[1]).sum(0)


def sum_everywhere(x):
    planes, along_z = group_lists()
    in_plane, depth = len(planes[0]), len(along_z[0])
    piece = sum_pieces(swap_pieces(x, planes), in_plane)
    piece = sum_pieces(swap_pieces(copies(piece, depth), along_z), depth)
    return swap_pieces(copies(piece, in_plane), planes)


def exact(a, b):
    return jnp.dot(a, b, precision=lax.Precision.HIGHEST, preferred_element_type=F32)


def weighted(weights, rows):
    total = None
    for w, r in zip(weights, rows):
        total = w * r if total is None else total + w * r
    return total


def stack(rows):
    part = lax.broadcasted_iota(jnp.int32, rows[0].shape, 0)
    out = rows[0]
    for i in range(1, len(rows)):
        out = jnp.where(part == i, rows[i], out)
    return out


def inverse_of_eight(panel, first):
    wide = panel.shape
    columns = [jnp.broadcast_to(panel[:, first + j : first + j + 1], wide) for j in range(8)]
    low = {(i, j): jnp.broadcast_to(columns[j][i : i + 1, :], wide) for j in range(8) for i in range(j, 8)}
    inv = {}
    for j in range(8):
        inv[j, j] = lax.rsqrt(low[j, j])
        for i in range(j + 1, 8):
            low[i, j] = low[i, j] * inv[j, j]
        for k in range(j + 1, 8):
            for i in range(k, 8):
                low[i, k] = low[i, k] - low[i, j] * low[k, j]
        for k in range(j):
            inv[j, k] = -inv[j, j] * weighted([low[j, m] for m in range(k, j)], [inv[m, k] for m in range(k, j)])
    return inv


def finish_body(scale, total_ref, own_ref, ortho_out, projected_out, inverse_ref):
    size = total_ref.shape[1]
    block = 32
    schur = total_ref[0:size, :] * scale
    at = lax.broadcasted_iota(jnp.int32, (size, size), 0)
    beside = (at == lax.broadcasted_iota(jnp.int32, (size, size), 1)).astype(F32)
    for start in range(0, size, block):
        here = [schur[i : i + 8] for i in range(0, block, 8)]
        here_beside = [beside[i : i + 8] for i in range(0, block, 8)]
        done, done_beside = [], []
        for p in range(block // 8):
            first = start + 8 * p
            top, top_beside = here[p], here_beside[p]
            inv = inverse_of_eight(top, first)
            rows = [jnp.broadcast_to(top[i : i + 1], top.shape) for i in range(8)]
            rows_beside = [jnp.broadcast_to(top_beside[i : i + 1], top.shape) for i in range(8)]
            solved = [weighted([inv[i, k] for k in range(i + 1)], rows) for i in range(8)]
            solved_beside = [weighted([inv[i, k] for k in range(i + 1)], rows_beside) for i in range(8)]
            done.append(stack(solved))
            done_beside.append(stack(solved_beside))
            inverse_ref[first : first + 8, :] = done_beside[-1]
            if p + 1 < block // 8:
                twice = [weighted([inv[k, i] for k in range(i, 8)], solved[i:]) for i in range(8)]
                twice_beside = [weighted([inv[k, i] for k in range(i, 8)], solved_beside[i:]) for i in range(8)]
            for q in range(p + 1, block // 8):
                columns = [jnp.broadcast_to(here[q][:, first + j : first + j + 1], top.shape) for j in range(8)]
                here[q] = here[q] - weighted(columns, twice)
                here_beside[q] = here_beside[q] - weighted(columns, twice_beside)
        if start + block < size:
            solved = jnp.concatenate(done, axis=0)
            both = jnp.concatenate([solved, jnp.concatenate(done_beside, axis=0)], axis=1)
            taken = exact(solved.T[start + block :], both)
            schur = schur[block:] - taken[:, 0:size]
            beside = beside[block:] - taken[:, size:]
    inverse = inverse_ref[...]
    coarse = inverse.astype(BF16)
    rest = inverse - coarse.astype(F32)
    fine = rest.astype(BF16)
    finest = (rest - fine.astype(F32)).astype(BF16)
    own = own_ref[...]
    ortho_out[...] = nn(coarse, own) + (nn(fine, own) + nn(finest, own))
    half_solved = exact(inverse, total_ref[size : 2 * size, :] * scale)
    projected_out[...] = lax.dot_general(
        half_solved, inverse, (((1,), (1,)), ((), ())), precision=lax.Precision.HIGHEST, preferred_element_type=F32
    )


def finish(scale, total, own_part):
    states, nodes = own_part.shape
    return pl.pallas_call(
        lambda *refs: finish_body(scale, *refs),
        out_shape=(jax.ShapeDtypeStruct((states, nodes), F32), jax.ShapeDtypeStruct((states, states), F32)),
        in_specs=[spec()] * 2,
        out_specs=(spec(), spec()),
        scratch_shapes=[pltpu.VMEM((states, states), F32)],
        compiler_params=pltpu.CompilerParams(vmem_limit_bytes=32 * MIB),
        name="finish",
    )(total, own_part)


def shards(block, cell_nodes, send_lists, cell_matrix, cell_scale, potential):
    lists = send_lists[0]
    own, slots = block.shape[1], lists.shape[1]
    full = own + 2 * slots
    states_here = block.shape[0]
    states = 2 * states_here
    band = lax.axis_index("band").astype(jnp.int32).reshape(1)
    potential = potential.reshape(1, own)

    to_left, to_right = send_first(block, lists)
    to_left, to_right, cell_nodes = lax.optimization_barrier((to_left, to_right, cell_nodes))
    from_left = shift(to_right, "dom", 1)
    from_right = shift(to_left, "dom", -1)
    mine = build(band, cell_nodes, cell_matrix, cell_scale, full)
    mine, from_left, from_right = lax.optimization_barrier((mine, from_left, from_right))
    other = lax.ppermute(mine, "band", [(0, 1), (1, 0)])
    x_here = jnp.concatenate([block, from_left[:states_here], from_right[:states_here]], axis=1)
    x0 = lax.all_gather(x_here, "band", axis=0, tiled=True)

    shapes = apply_shapes(states, own, slots)
    x_shape = jax.ShapeDtypeStruct((states, full), BF16)
    fixed = (band, mine, other, potential, lists)
    ends = fixed + (from_left, from_right)
    partial, ghost, near, far = stage_call(first_body, fixed + (x0,), shapes, "apply_one")
    got = exchange(near, far)
    x1, partial, ghost, near, far = stage_call(
        lambda *r: next_body(False, *r), ends + (partial, ghost, got), (x_shape,) + shapes, "apply_two"
    )
    got = exchange(near, far)
    x2, partial, ghost, near, far = stage_call(
        lambda *r: next_body(True, *r), ends + (partial, ghost, got, x0), (x_shape,) + shapes, "apply_three"
    )
    got = exchange(near, far)
    own_part, sums = stage_call(
        last_body,
        ends + (partial, ghost, got, x1),
        (jax.ShapeDtypeStruct((states, own // 2), BF16), jax.ShapeDtypeStruct((2 * states, states), F32)),
        "apply_four",
        (pltpu.VMEM((states, full), BF16), pltpu.VMEM((1, own), F32)),
    )
    return finish(1.0 / (own * lax.axis_size("dom")), sum_everywhere(sums), own_part)


def solution(mesh):
    return jax.shard_map(
        shards,
        mesh=mesh,
        in_specs=(P("band", "dom"), P("dom", None), P("dom", None, None), P(), P("dom"), P("dom")),
        out_specs=(P(None, ("dom", "band")), P()),
        check_vma=False,
    )
```

```python
import jax
import jax.numpy as jnp
from jax import lax
from jax.experimental import pallas as pl
from jax.experimental.pallas import tpu as pltpu
from jax.sharding import PartitionSpec as P

BOTH = ("dom", "band")
BF16 = jnp.bfloat16
F32 = jnp.float32
CELL_PAD = 128
MIB = 1 << 20


def spec(space=pltpu.VMEM):
    return pl.BlockSpec(memory_space=space)


def nn(a, b):
    return lax.dot_general(a, b, (((1,), (0,)), ((), ())), preferred_element_type=F32)


def nt(a, b):
    return lax.dot_general(a, b, (((1,), (1,)), ((), ())), preferred_element_type=F32)


def one_hot(rows, row):
    hit = lax.broadcasted_iota(row.dtype, (rows, row.shape[1]), 0) == row
    return hit.astype(F32).astype(BF16)


def pair_mask(column, row):
    return (column == row).astype(F32).astype(BF16)


def send_body(block_ref, lists_ref, left_ref, right_ref):
    own = block_ref.shape[1]
    states = block_ref.shape[0]
    lists = lists_ref[...]
    slots = lists.shape[1]
    part = lax.broadcasted_iota(jnp.int32, (16, slots), 0)
    codes = jnp.zeros((16, slots), jnp.int32)
    for side in (0, 1):
        one = lists[side : side + 1]
        codes = jnp.where(part == 2 * side, one >> 5, codes)
        codes = jnp.where(part == 2 * side + 1, one & 31, codes)
    codes = codes.astype(F32).astype(BF16)
    for side, out in ((0, left_ref), (1, right_ref)):
        out[0:states, :] = nn(block_ref[...], one_hot(own, lists[side : side + 1])).astype(BF16)
        out[states : states + 16, :] = codes


def send_first(block, lists):
    states, slots = block.shape[0], lists.shape[1]
    shape = jax.ShapeDtypeStruct((states + 16, slots), BF16)
    return pl.pallas_call(
        send_body,
        out_shape=(shape, shape),
        in_specs=[spec()] * 2,
        out_specs=(spec(), spec()),
        name="send_first",
    )(block, lists)


def build_body(band_ref, packed_ref, out_ref, hot, left):
    half, full = out_ref.shape
    cells = left.shape[1] // CELL_PAD
    first = band_ref[0] * half
    matrix = packed_ref[cells : cells + CELL_PAD, :].T
    nothing = jnp.zeros((CELL_PAD, CELL_PAD), F32)
    pair_matrix = jnp.concatenate(
        [jnp.concatenate([matrix, nothing], axis=1), jnp.concatenate([nothing, matrix], axis=1)], axis=0
    ).astype(BF16)
    for pair in range(cells // 2):
        both = (2 * pair, 2 * pair + 1)
        row = jnp.concatenate([packed_ref[c : c + 1, :] for c in both], axis=1).astype(jnp.int32)
        at = cells + CELL_PAD
        gain = [jnp.broadcast_to(packed_ref[at : at + 1, c : c + 1], (1, CELL_PAD)) for c in both]
        cols = slice(pair * 2 * CELL_PAD, (pair + 1) * 2 * CELL_PAD)
        product = nn(one_hot(half, row - first), pair_matrix)
        left[:, cols] = (product * jnp.concatenate(gain, axis=1)).astype(BF16)
        hot[:, cols] = one_hot(full, row)
    for at in range(0, half, 256):
        out_ref[at : at + 256, :] = nt(left[at : at + 256, :], hot[...]).astype(BF16)


def build(band, cell_nodes, cell_matrix, cell_scale, full):
    cells, nodes = cell_nodes.shape
    half = full // 2
    entries = cells * CELL_PAD
    spare = CELL_PAD - nodes
    packed = jnp.concatenate(
        [
            jnp.pad(cell_nodes.astype(F32), ((0, 0), (0, spare)), constant_values=-8192.0),
            jnp.pad(cell_matrix.astype(F32), ((0, spare), (0, spare))),
            jnp.pad(cell_scale[None], ((0, 7), (0, CELL_PAD - cells))),
        ],
        axis=0,
    )
    return pl.pallas_call(
        build_body,
        out_shape=jax.ShapeDtypeStruct((half, full), BF16),
        in_specs=[spec(pltpu.SMEM), spec()],
        out_specs=spec(),
        scratch_shapes=[pltpu.VMEM((full, entries), BF16), pltpu.VMEM((half, entries), BF16)],
        compiler_params=pltpu.CompilerParams(vmem_limit_bytes=44 * MIB),
        cost_estimate=pl.CostEstimate(
            flops=2 * half * entries * full, bytes_accessed=2 * half * full, transcendentals=0
        ),
        name="build",
    )(band, packed)


def decode(codes_ref):
    slots = codes_ref.shape[1]
    codes = codes_ref[codes_ref.shape[0] - 16 :, :].astype(F32)
    rows = [codes[2 * s : 2 * s + 1] * 32.0 + codes[2 * s + 1 : 2 * s + 2] for s in (0, 1)]
    part = lax.broadcasted_iota(jnp.int32, (8, slots), 0)
    both = jnp.where(part == 0, rows[0], rows[1])
    columns = both.T
    return rows, [columns[:, 0:1], columns[:, 1:2]]


def assemble(band_ref, partial_ref, ghost_ref, got_ref, lists, from_left_ref, from_right_ref, own):
    slots = lists.shape[1]
    (left_rows, left_cols), (right_rows, right_cols) = decode(from_left_ref), decode(from_right_ref)
    ghost = ghost_ref[...]
    ghost_left, ghost_right = ghost[:, 0:slots], ghost[:, slots : 2 * slots]
    states = ghost.shape[0]
    got_left, got_right = got_ref[0:states, :], got_ref[states : 2 * states, :]
    near_left, near_right = got_left[:, 0:slots], got_right[:, 0:slots]
    far_left, far_right = (
        jnp.where(band_ref[1 + side] == 1, got[:, 2 * slots : 3 * slots], jnp.zeros((states, slots), BF16))
        for side, got in ((0, got_left), (1, got_right))
    )
    whole_own = (
        partial_ref[...]
        + nt(near_left, one_hot(own, lists[0:1]))
        + nt(near_right, one_hot(own, lists[1:2]))
    )
    whole_left = (
        got_left[:, slots : 2 * slots].astype(F32)
        + nn(far_left, pair_mask(left_cols[0], left_rows[1]))
        + nn(ghost_left, pair_mask(left_cols[1], left_rows[1]))
    )
    whole_right = (
        got_right[:, slots : 2 * slots].astype(F32)
        + nn(far_right, pair_mask(right_cols[1], right_rows[0]))
        + nn(ghost_right, pair_mask(right_cols[0], right_rows[0]))
    )
    return whole_own, whole_left, whole_right


def times_operator(band, x_ref, mine_ref, other_ref, cols):
    half = mine_ref.shape[0]
    here = pl.ds(pl.multiple_of(band * half, 128), half)
    there = pl.ds(pl.multiple_of((1 - band) * half, 128), half)
    return nn(x_ref[:, here], mine_ref[:, cols]) + nn(x_ref[:, there], other_ref[:, cols])


def apply_body(
    band_ref, x_ref, mine_ref, other_ref, potential_ref, lists, partial_out, ghost_out, near_out, far_out
):
    own = partial_out.shape[1]
    slots = lists.shape[1]
    result = times_operator(band_ref[0], x_ref, mine_ref, other_ref, slice(None))
    partial = result[:, 0:own] + potential_ref[...] * x_ref[:, 0:own].astype(F32)
    partial_out[...] = partial
    ghost = result[:, own:].astype(BF16)
    ghost_out[...] = ghost
    right = band_ref[0] == 1
    mine = jnp.where(right, lists[1:2], lists[0:1])
    edge = jnp.where(right, ghost[:, slots : 2 * slots], ghost[:, 0:slots])
    near_out[:, 0:slots] = edge
    near_out[:, slots : 2 * slots] = nn(partial.astype(BF16), one_hot(own, mine)).astype(BF16)
    far_out[...] = edge


def first_body(band_ref, mine_ref, other_ref, potential_ref, lists_ref, x_ref, *outs):
    apply_body(band_ref, x_ref, mine_ref, other_ref, potential_ref, lists_ref[...], *outs)


def new_states(older_ref, x_out, pieces):
    own = pieces[0].shape[1]
    slots = pieces[1].shape[1]
    at = 0
    for piece in pieces:
        cols = slice(at, at + piece.shape[1])
        if older_ref is not None:
            piece = 2.0 * piece - older_ref[:, cols].astype(F32)
        x_out[:, cols] = piece.astype(BF16)
        at += piece.shape[1]


def next_body(chebyshev, *refs):
    band_ref, mine_ref, other_ref, potential_ref, lists_ref, fl_ref, fr_ref, partial_ref, ghost_ref, got_ref = refs[:10]
    older_ref = refs[10] if chebyshev else None
    x_out, *outs = refs[11:] if chebyshev else refs[10:]
    lists = lists_ref[...]
    own = partial_ref.shape[1]
    new_states(older_ref, x_out, assemble(band_ref, partial_ref, ghost_ref, got_ref, lists, fl_ref, fr_ref, own))
    apply_body(band_ref, x_out, mine_ref, other_ref, potential_ref, lists, *outs)


def last_body(
    band_ref, mine_ref, other_ref, potential_ref, lists_ref, fl_ref, fr_ref, partial_ref, ghost_ref, got_ref,
    older_ref, own_out, sums_out, x_all, pot,
):
    lists = lists_ref[...]
    own = partial_ref.shape[1]
    states = partial_ref.shape[0]
    slots = lists.shape[1]
    new_states(older_ref, x_all, assemble(band_ref, partial_ref, ghost_ref, got_ref, lists, fl_ref, fr_ref, own))
    pot[...] = potential_ref[...]
    half = own // 2
    mine = pl.ds(pl.multiple_of(band_ref[0] * half, 128), half)
    edge = pl.ds(pl.multiple_of(own + band_ref[0] * slots, 128), slots)
    x_mine = x_all[:, mine]
    own_out[...] = x_mine
    sums_out[0:states, :] = nt(x_mine, x_mine)
    image = times_operator(band_ref[0], x_all, mine_ref, other_ref, mine) + pot[:, mine] * x_mine.astype(F32)
    image_edge = times_operator(band_ref[0], x_all, mine_ref, other_ref, edge)
    sums_out[states : 2 * states, :] = nt(x_mine, image.astype(BF16)) + nt(x_all[:, edge], image_edge.astype(BF16))


def apply_shapes(states, own, slots):
    return (
        jax.ShapeDtypeStruct((states, own), F32),
        jax.ShapeDtypeStruct((states, 2 * slots), BF16),
        jax.ShapeDtypeStruct((states, 2 * slots), BF16),
        jax.ShapeDtypeStruct((states, slots), BF16),
    )


def stage_call(body, args, shapes, name, scratch=()):
    return pl.pallas_call(
        body,
        out_shape=tuple(shapes),
        in_specs=[spec(pltpu.SMEM)] + [spec()] * (len(args) - 1),
        out_specs=tuple(spec() for _ in shapes),
        scratch_shapes=list(scratch),
        compiler_params=pltpu.CompilerParams(vmem_limit_bytes=32 * MIB),
        name=name,
    )(*args)


def shift(x, axis, by):
    devices = lax.axis_size(axis)
    return lax.ppermute(x, axis, [(i, i + by) for i in range(devices) if 0 <= i + by < devices])


def across(x, by):
    parts = lax.axis_size("dom")
    pairs = [(2 * d + 1, 2 * (d + by)) for d in range(parts - by)]
    pairs += [(2 * (d + by), 2 * d + 1) for d in range(parts - by)]
    return lax.ppermute(x, BOTH, pairs)


def far_groups(parts):
    pairs = [[2 * d + 1, 2 * d + 4] for d in range(parts - 2)]
    return pairs + [[0, 2], [2 * parts - 3, 2 * parts - 1]]


def exchange(band, near, far):
    rows = far.shape[0]
    near = across(near, 1)
    both = lax.all_gather(far, BOTH, axis_index_groups=far_groups(lax.axis_size("dom")), axis=0, tiled=True)
    far = lax.dynamic_slice_in_dim(both, band * rows, rows, 0)
    return lax.all_gather(jnp.concatenate([near, far], axis=1), "band", axis=0, tiled=True)


def group_lists():
    planes, along_z = {}, {}
    for x in range(4):
        for z in range(16):
            for y in range(4):
                for b in range(2):
                    i = ((x * 16 + z) * 4 + y) * 2 + b
                    planes.setdefault(z, []).append(i)
                    along_z.setdefault((x, y, b), []).append(i)
    return list(planes.values()), list(along_z.values())


def swap_pieces(x, groups):
    return lax.all_to_all(x, BOTH, 0, 0, axis_index_groups=groups, tiled=True)


def copies(piece, count):
    return jnp.broadcast_to(piece[None], (count,) + piece.shape).reshape(count * piece.shape[0], piece.shape[1])


def sum_pieces(x, count):
    return x.reshape(count, x.shape[0] // count, x.shape[1]).sum(0)


def sum_everywhere(x):
    planes, along_z = group_lists()
    in_plane, depth = len(planes[0]), len(along_z[0])
    piece = sum_pieces(swap_pieces(x, planes), in_plane)
    piece = sum_pieces(swap_pieces(copies(piece, depth), along_z), depth)
    return swap_pieces(copies(piece, in_plane), planes)


def exact(a, b):
    return jnp.dot(a, b, precision=lax.Precision.HIGHEST, preferred_element_type=F32)


def weighted(weights, rows):
    total = None
    for w, r in zip(weights, rows):
        total = w * r if total is None else total + w * r
    return total


def stack(rows):
    part = lax.broadcasted_iota(jnp.int32, rows[0].shape, 0)
    out = rows[0]
    for i in range(1, len(rows)):
        out = jnp.where(part == i, rows[i], out)
    return out


def inverse_of_eight(panel, first):
    wide = panel.shape
    columns = [jnp.broadcast_to(panel[:, first + j : first + j + 1], wide) for j in range(8)]
    low = {(i, j): jnp.broadcast_to(columns[j][i : i + 1, :], wide) for j in range(8) for i in range(j, 8)}
    inv = {}
    for j in range(8):
        inv[j, j] = lax.rsqrt(low[j, j])
        for i in range(j + 1, 8):
            low[i, j] = low[i, j] * inv[j, j]
        for k in range(j + 1, 8):
            for i in range(k, 8):
                low[i, k] = low[i, k] - low[i, j] * low[k, j]
        for k in range(j):
            inv[j, k] = -inv[j, j] * weighted([low[j, m] for m in range(k, j)], [inv[m, k] for m in range(k, j)])
    return inv


def finish_body(scale, total_ref, own_ref, ortho_out, projected_out, inverse_ref):
    size = total_ref.shape[1]
    block = 32
    schur = total_ref[0:size, :] * scale
    at = lax.broadcasted_iota(jnp.int32, (size, size), 0)
    beside = (at == lax.broadcasted_iota(jnp.int32, (size, size), 1)).astype(F32)
    for start in range(0, size, block):
        here = [schur[i : i + 8] for i in range(0, block, 8)]
        here_beside = [beside[i : i + 8] for i in range(0, block, 8)]
        done, done_beside = [], []
        for p in range(block // 8):
            first = start + 8 * p
            top, top_beside = here[p], here_beside[p]
            inv = inverse_of_eight(top, first)
            rows = [jnp.broadcast_to(top[i : i + 1], top.shape) for i in range(8)]
            rows_beside = [jnp.broadcast_to(top_beside[i : i + 1], top.shape) for i in range(8)]
            solved = [weighted([inv[i, k] for k in range(i + 1)], rows) for i in range(8)]
            solved_beside = [weighted([inv[i, k] for k in range(i + 1)], rows_beside) for i in range(8)]
            done.append(stack(solved))
            done_beside.append(stack(solved_beside))
            inverse_ref[first : first + 8, :] = done_beside[-1]
            if p + 1 < block // 8:
                twice = [weighted([inv[k, i] for k in range(i, 8)], solved[i:]) for i in range(8)]
                twice_beside = [weighted([inv[k, i] for k in range(i, 8)], solved_beside[i:]) for i in range(8)]
            for q in range(p + 1, block // 8):
                columns = [jnp.broadcast_to(here[q][:, first + j : first + j + 1], top.shape) for j in range(8)]
                here[q] = here[q] - weighted(columns, twice)
                here_beside[q] = here_beside[q] - weighted(columns, twice_beside)
        if start + block < size:
            solved = jnp.concatenate(done, axis=0)
            both = jnp.concatenate([solved, jnp.concatenate(done_beside, axis=0)], axis=1)
            taken = exact(solved.T[start + block :], both)
            schur = schur[block:] - taken[:, 0:size]
            beside = beside[block:] - taken[:, size:]
    inverse = inverse_ref[...]
    coarse = inverse.astype(BF16)
    rest = inverse - coarse.astype(F32)
    fine = rest.astype(BF16)
    finest = (rest - fine.astype(F32)).astype(BF16)
    own = own_ref[...]
    ortho_out[...] = nn(coarse, own) + (nn(fine, own) + nn(finest, own))
    half_solved = exact(inverse, total_ref[size : 2 * size, :] * scale)
    projected_out[...] = lax.dot_general(
        half_solved, inverse, (((1,), (1,)), ((), ())), precision=lax.Precision.HIGHEST, preferred_element_type=F32
    )


def finish(scale, total, own_part):
    states, nodes = own_part.shape
    return pl.pallas_call(
        lambda *refs: finish_body(scale, *refs),
        out_shape=(jax.ShapeDtypeStruct((states, nodes), F32), jax.ShapeDtypeStruct((states, states), F32)),
        in_specs=[spec()] * 2,
        out_specs=(spec(), spec()),
        scratch_shapes=[pltpu.VMEM((states, states), F32)],
        compiler_params=pltpu.CompilerParams(vmem_limit_bytes=32 * MIB),
        name="finish",
    )(total, own_part)


def shards(block, cell_nodes, send_lists, cell_matrix, cell_scale, potential):
    lists = send_lists[0]
    own, slots = block.shape[1], lists.shape[1]
    full = own + 2 * slots
    states_here = block.shape[0]
    states = 2 * states_here
    core, part = lax.axis_index("band"), lax.axis_index("dom")
    band = jnp.stack([core, part >= 2, part < lax.axis_size("dom") - 2]).astype(jnp.int32)
    potential = potential.reshape(1, own)

    to_left, to_right = send_first(block, lists)
    to_left, to_right, cell_nodes = lax.optimization_barrier((to_left, to_right, cell_nodes))
    from_left = shift(to_right, "dom", 1)
    from_right = shift(to_left, "dom", -1)
    mine = build(band, cell_nodes, cell_matrix, cell_scale, full)
    mine, from_left, from_right = lax.optimization_barrier((mine, from_left, from_right))
    other = lax.ppermute(mine, "band", [(0, 1), (1, 0)])
    x_here = jnp.concatenate([block, from_left[:states_here], from_right[:states_here]], axis=1)
    x0 = lax.all_gather(x_here, "band", axis=0, tiled=True)

    shapes = apply_shapes(states, own, slots)
    x_shape = jax.ShapeDtypeStruct((states, full), BF16)
    fixed = (band, mine, other, potential, lists)
    ends = fixed + (from_left, from_right)
    partial, ghost, near, far = stage_call(first_body, fixed + (x0,), shapes, "apply_one")
    got = exchange(core, near, far)
    x1, partial, ghost, near, far = stage_call(
        lambda *r: next_body(False, *r), ends + (partial, ghost, got), (x_shape,) + shapes, "apply_two"
    )
    got = exchange(core, near, far)
    x2, partial, ghost, near, far = stage_call(
        lambda *r: next_body(True, *r), ends + (partial, ghost, got, x0), (x_shape,) + shapes, "apply_three"
    )
    got = exchange(core, near, far)
    own_part, sums = stage_call(
        last_body,
        ends + (partial, ghost, got, x1),
        (jax.ShapeDtypeStruct((states, own // 2), BF16), jax.ShapeDtypeStruct((2 * states, states), F32)),
        "apply_four",
        (pltpu.VMEM((states, full), BF16), pltpu.VMEM((1, own), F32)),
    )
    return finish(1.0 / (own * lax.axis_size("dom")), sum_everywhere(sums), own_part)


def solution(mesh):
    return jax.shard_map(
        shards,
        mesh=mesh,
        in_specs=(P("band", "dom"), P("dom", None), P("dom", None, None), P(), P("dom"), P("dom")),
        out_specs=(P(None, ("dom", "band")), P()),
        check_vma=False,
    )
```

```python
import jax
import jax.numpy as jnp
from jax import lax
from jax.experimental import pallas as pl
from jax.experimental.pallas import tpu as pltpu
from jax.sharding import PartitionSpec as P

BOTH = ("dom", "band")
BF16 = jnp.bfloat16
F32 = jnp.float32
CELL_PAD = 128
MIB = 1 << 20


def spec(space=pltpu.VMEM):
    return pl.BlockSpec(memory_space=space)


def nn(a, b):
    return lax.dot_general(a, b, (((1,), (0,)), ((), ())), preferred_element_type=F32)


def nt(a, b):
    return lax.dot_general(a, b, (((1,), (1,)), ((), ())), preferred_element_type=F32)


def one_hot(rows, row):
    hit = lax.broadcasted_iota(row.dtype, (rows, row.shape[1]), 0) == row
    return hit.astype(F32).astype(BF16)


def pair_mask(column, row):
    return (column == row).astype(F32).astype(BF16)


def send_body(block_ref, lists_ref, left_ref, right_ref):
    own = block_ref.shape[1]
    states = block_ref.shape[0]
    lists = lists_ref[...]
    slots = lists.shape[1]
    part = lax.broadcasted_iota(jnp.int32, (16, slots), 0)
    codes = jnp.zeros((16, slots), jnp.int32)
    for side in (0, 1):
        one = lists[side : side + 1]
        codes = jnp.where(part == 2 * side, one >> 5, codes)
        codes = jnp.where(part == 2 * side + 1, one & 31, codes)
    codes = codes.astype(F32).astype(BF16)
    for side, out in ((0, left_ref), (1, right_ref)):
        out[0:states, :] = nn(block_ref[...], one_hot(own, lists[side : side + 1])).astype(BF16)
        out[states : states + 16, :] = codes


def send_first(block, lists):
    states, slots = block.shape[0], lists.shape[1]
    shape = jax.ShapeDtypeStruct((states + 16, slots), BF16)
    return pl.pallas_call(
        send_body,
        out_shape=(shape, shape),
        in_specs=[spec()] * 2,
        out_specs=(spec(), spec()),
        name="send_first",
    )(block, lists)


def build_body(band_ref, packed_ref, out_ref, hot, left):
    half, full = out_ref.shape
    cells = left.shape[1] // CELL_PAD
    first = band_ref[0] * half
    matrix = packed_ref[cells : cells + CELL_PAD, :].T
    nothing = jnp.zeros((CELL_PAD, CELL_PAD), F32)
    pair_matrix = jnp.concatenate(
        [jnp.concatenate([matrix, nothing], axis=1), jnp.concatenate([nothing, matrix], axis=1)], axis=0
    ).astype(BF16)
    for pair in range(cells // 2):
        both = (2 * pair, 2 * pair + 1)
        row = jnp.concatenate([packed_ref[c : c + 1, :] for c in both], axis=1).astype(jnp.int32)
        at = cells + CELL_PAD
        gain = [jnp.broadcast_to(packed_ref[at : at + 1, c : c + 1], (1, CELL_PAD)) for c in both]
        cols = slice(pair * 2 * CELL_PAD, (pair + 1) * 2 * CELL_PAD)
        product = nn(one_hot(half, row - first), pair_matrix)
        left[:, cols] = (product * jnp.concatenate(gain, axis=1)).astype(BF16)
        hot[:, cols] = one_hot(full, row)
    for at in range(0, half, 256):
        out_ref[at : at + 256, :] = nt(left[at : at + 256, :], hot[...]).astype(BF16)


def build(band, cell_nodes, cell_matrix, cell_scale, full):
    cells, nodes = cell_nodes.shape
    half = full // 2
    entries = cells * CELL_PAD
    spare = CELL_PAD - nodes
    packed = jnp.concatenate(
        [
            jnp.pad(cell_nodes.astype(F32), ((0, 0), (0, spare)), constant_values=-8192.0),
            jnp.pad(cell_matrix.astype(F32), ((0, spare), (0, spare))),
            jnp.pad(cell_scale[None], ((0, 7), (0, CELL_PAD - cells))),
        ],
        axis=0,
    )
    return pl.pallas_call(
        build_body,
        out_shape=jax.ShapeDtypeStruct((half, full), BF16),
        in_specs=[spec(pltpu.SMEM), spec()],
        out_specs=spec(),
        scratch_shapes=[pltpu.VMEM((full, entries), BF16), pltpu.VMEM((half, entries), BF16)],
        compiler_params=pltpu.CompilerParams(vmem_limit_bytes=26 * MIB),
        cost_estimate=pl.CostEstimate(
            flops=2 * half * entries * full, bytes_accessed=2 * half * full, transcendentals=0
        ),
        name="build",
    )(band, packed)


def decode(codes_ref):
    slots = codes_ref.shape[1]
    codes = codes_ref[codes_ref.shape[0] - 16 :, :].astype(F32)
    rows = [codes[2 * s : 2 * s + 1] * 32.0 + codes[2 * s + 1 : 2 * s + 2] for s in (0, 1)]
    part = lax.broadcasted_iota(jnp.int32, (8, slots), 0)
    both = jnp.where(part == 0, rows[0], rows[1])
    columns = both.T
    return rows, [columns[:, 0:1], columns[:, 1:2]]


def assemble(band_ref, partial_ref, ghost_ref, got_ref, lists, from_left_ref, from_right_ref, own):
    slots = lists.shape[1]
    (left_rows, left_cols), (right_rows, right_cols) = decode(from_left_ref), decode(from_right_ref)
    ghost = ghost_ref[...]
    ghost_left, ghost_right = ghost[:, 0:slots], ghost[:, slots : 2 * slots]
    states = ghost.shape[0]
    got_left, got_right = got_ref[0:states, :], got_ref[states : 2 * states, :]
    near_left, near_right = got_left[:, 0:slots], got_right[:, 0:slots]
    far_left, far_right = (
        jnp.where(band_ref[1 + side] == 1, got[:, 2 * slots : 3 * slots], jnp.zeros((states, slots), BF16))
        for side, got in ((0, got_left), (1, got_right))
    )
    whole_own = (
        partial_ref[...]
        + nt(near_left, one_hot(own, lists[0:1]))
        + nt(near_right, one_hot(own, lists[1:2]))
    )
    whole_left = (
        got_left[:, slots : 2 * slots].astype(F32)
        + nn(far_left, pair_mask(left_cols[0], left_rows[1]))
        + nn(ghost_left, pair_mask(left_cols[1], left_rows[1]))
    )
    whole_right = (
        got_right[:, slots : 2 * slots].astype(F32)
        + nn(far_right, pair_mask(right_cols[1], right_rows[0]))
        + nn(ghost_right, pair_mask(right_cols[0], right_rows[0]))
    )
    return whole_own, whole_left, whole_right


def times_half(which, x_ref, w_ref, cols):
    half = w_ref.shape[0]
    return nn(x_ref[:, pl.ds(pl.multiple_of(which * half, 128), half)], w_ref[:, cols])


def times_operator(band, x_ref, mine_ref, other_ref, cols):
    return times_half(band, x_ref, mine_ref, cols) + times_half(1 - band, x_ref, other_ref, cols)


def apply_body(band_ref, x_ref, mine_ref, other_ref, *refs):
    give(band_ref, times_operator(band_ref[0], x_ref, mine_ref, other_ref, slice(None)), x_ref, *refs)


def give(band_ref, result, x_ref, potential_ref, lists, partial_out, ghost_out, near_out, far_out):
    own = partial_out.shape[1]
    slots = lists.shape[1]
    partial = result[:, 0:own] + potential_ref[...] * x_ref[:, 0:own].astype(F32)
    partial_out[...] = partial
    ghost = result[:, own:].astype(BF16)
    ghost_out[...] = ghost
    right = band_ref[0] == 1
    mine = jnp.where(right, lists[1:2], lists[0:1])
    edge = jnp.where(right, ghost[:, slots : 2 * slots], ghost[:, 0:slots])
    near_out[:, 0:slots] = edge
    near_out[:, slots : 2 * slots] = nn(partial.astype(BF16), one_hot(own, mine)).astype(BF16)
    far_out[...] = edge


def first_body(
    band_ref, mine_ref, other_hbm, potential_ref, lists_ref, x_ref, other_out, partial_out, ghost_out, near_out,
    far_out, sem,
):
    arrival = pltpu.make_async_copy(other_hbm, other_out, sem)
    arrival.start()
    result = times_half(band_ref[0], x_ref, mine_ref, slice(None))
    arrival.wait()
    result = result + times_half(1 - band_ref[0], x_ref, other_out, slice(None))
    give(band_ref, result, x_ref, potential_ref, lists_ref[...], partial_out, ghost_out, near_out, far_out)


def new_states(older_ref, x_out, pieces):
    own = pieces[0].shape[1]
    slots = pieces[1].shape[1]
    at = 0
    for piece in pieces:
        cols = slice(at, at + piece.shape[1])
        if older_ref is not None:
            piece = 2.0 * piece - older_ref[:, cols].astype(F32)
        x_out[:, cols] = piece.astype(BF16)
        at += piece.shape[1]


def next_body(chebyshev, *refs):
    band_ref, mine_ref, other_ref, potential_ref, lists_ref, fl_ref, fr_ref, partial_ref, ghost_ref, got_ref = refs[:10]
    older_ref = refs[10] if chebyshev else None
    x_out, *outs = refs[11:] if chebyshev else refs[10:]
    lists = lists_ref[...]
    own = partial_ref.shape[1]
    new_states(older_ref, x_out, assemble(band_ref, partial_ref, ghost_ref, got_ref, lists, fl_ref, fr_ref, own))
    apply_body(band_ref, x_out, mine_ref, other_ref, potential_ref, lists, *outs)


def last_body(
    band_ref, mine_ref, other_ref, potential_ref, lists_ref, fl_ref, fr_ref, partial_ref, ghost_ref, got_ref,
    older_ref, own_out, sums_out, x_all, pot,
):
    lists = lists_ref[...]
    own = partial_ref.shape[1]
    states = partial_ref.shape[0]
    slots = lists.shape[1]
    new_states(older_ref, x_all, assemble(band_ref, partial_ref, ghost_ref, got_ref, lists, fl_ref, fr_ref, own))
    pot[...] = potential_ref[...]
    half = own // 2
    mine = pl.ds(pl.multiple_of(band_ref[0] * half, 128), half)
    edge = pl.ds(pl.multiple_of(own + band_ref[0] * slots, 128), slots)
    x_mine = x_all[:, mine]
    own_out[...] = x_mine
    sums_out[0:states, :] = nt(x_mine, x_mine)
    image = times_operator(band_ref[0], x_all, mine_ref, other_ref, mine) + pot[:, mine] * x_mine.astype(F32)
    image_edge = times_operator(band_ref[0], x_all, mine_ref, other_ref, edge)
    sums_out[states : 2 * states, :] = nt(x_mine, image.astype(BF16)) + nt(x_all[:, edge], image_edge.astype(BF16))


def apply_shapes(states, own, slots):
    return (
        jax.ShapeDtypeStruct((states, own), F32),
        jax.ShapeDtypeStruct((states, 2 * slots), BF16),
        jax.ShapeDtypeStruct((states, 2 * slots), BF16),
        jax.ShapeDtypeStruct((states, slots), BF16),
    )


def stage_call(body, args, shapes, name, scratch=(), anywhere=()):
    return pl.pallas_call(
        body,
        out_shape=tuple(shapes),
        in_specs=[spec(pltpu.SMEM)] + [spec(pl.ANY if i in anywhere else pltpu.VMEM) for i in range(1, len(args))],
        out_specs=tuple(spec() for _ in shapes),
        scratch_shapes=list(scratch),
        compiler_params=pltpu.CompilerParams(vmem_limit_bytes=16 * MIB),
        name=name,
    )(*args)


def shift(x, axis, by):
    devices = lax.axis_size(axis)
    return lax.ppermute(x, axis, [(i, i + by) for i in range(devices) if 0 <= i + by < devices])


def across(x, by):
    parts = lax.axis_size("dom")
    pairs = [(2 * d + 1, 2 * (d + by)) for d in range(parts - by)]
    pairs += [(2 * (d + by), 2 * d + 1) for d in range(parts - by)]
    return lax.ppermute(x, BOTH, pairs)


def far_groups(parts):
    pairs = [[2 * d + 1, 2 * d + 4] for d in range(parts - 2)]
    return pairs + [[0, 2], [2 * parts - 3, 2 * parts - 1]]


def exchange(band, near, far):
    rows = far.shape[0]
    near = across(near, 1)
    both = lax.all_gather(far, BOTH, axis_index_groups=far_groups(lax.axis_size("dom")), axis=0, tiled=True)
    far = lax.dynamic_slice_in_dim(both, band * rows, rows, 0)
    return lax.all_gather(jnp.concatenate([near, far], axis=1), "band", axis=0, tiled=True)


def group_lists():
    planes, along_z = {}, {}
    for x in range(4):
        for z in range(16):
            for y in range(4):
                for b in range(2):
                    i = ((x * 16 + z) * 4 + y) * 2 + b
                    planes.setdefault(z, []).append(i)
                    along_z.setdefault((x, y, b), []).append(i)
    return list(planes.values()), list(along_z.values())


def swap_pieces(x, groups):
    return lax.all_to_all(x, BOTH, 0, 0, axis_index_groups=groups, tiled=True)


def copies(piece, count):
    return jnp.broadcast_to(piece[None], (count,) + piece.shape).reshape(count * piece.shape[0], piece.shape[1])


def sum_pieces(x, count):
    return x.reshape(count, x.shape[0] // count, x.shape[1]).sum(0)


def sum_everywhere(x):
    planes, along_z = group_lists()
    in_plane, depth = len(planes[0]), len(along_z[0])
    piece = sum_pieces(swap_pieces(x, planes), in_plane)
    piece = sum_pieces(swap_pieces(copies(piece, depth), along_z), depth)
    return swap_pieces(copies(piece, in_plane), planes)


def exact(a, b):
    return jnp.dot(a, b, precision=lax.Precision.HIGHEST, preferred_element_type=F32)


def weighted(weights, rows):
    total = None
    for w, r in zip(weights, rows):
        total = w * r if total is None else total + w * r
    return total


def stack(rows):
    part = lax.broadcasted_iota(jnp.int32, rows[0].shape, 0)
    out = rows[0]
    for i in range(1, len(rows)):
        out = jnp.where(part == i, rows[i], out)
    return out


def inverse_of_eight(panel, first):
    wide = panel.shape
    columns = [jnp.broadcast_to(panel[:, first + j : first + j + 1], wide) for j in range(8)]
    low = {(i, j): jnp.broadcast_to(columns[j][i : i + 1, :], wide) for j in range(8) for i in range(j, 8)}
    inv = {}
    for j in range(8):
        inv[j, j] = lax.rsqrt(low[j, j])
        for i in range(j + 1, 8):
            low[i, j] = low[i, j] * inv[j, j]
        for k in range(j + 1, 8):
            for i in range(k, 8):
                low[i, k] = low[i, k] - low[i, j] * low[k, j]
        for k in range(j):
            inv[j, k] = -inv[j, j] * weighted([low[j, m] for m in range(k, j)], [inv[m, k] for m in range(k, j)])
    return inv


def finish_body(scale, total_ref, own_ref, ortho_out, projected_out, inverse_ref):
    size = total_ref.shape[1]
    block = 32
    schur = total_ref[0:size, :] * scale
    at = lax.broadcasted_iota(jnp.int32, (size, size), 0)
    beside = (at == lax.broadcasted_iota(jnp.int32, (size, size), 1)).astype(F32)
    for start in range(0, size, block):
        here = [schur[i : i + 8] for i in range(0, block, 8)]
        here_beside = [beside[i : i + 8] for i in range(0, block, 8)]
        done, done_beside = [], []
        for p in range(block // 8):
            first = start + 8 * p
            top, top_beside = here[p], here_beside[p]
            inv = inverse_of_eight(top, first)
            rows = [jnp.broadcast_to(top[i : i + 1], top.shape) for i in range(8)]
            rows_beside = [jnp.broadcast_to(top_beside[i : i + 1], top.shape) for i in range(8)]
            solved = [weighted([inv[i, k] for k in range(i + 1)], rows) for i in range(8)]
            solved_beside = [weighted([inv[i, k] for k in range(i + 1)], rows_beside) for i in range(8)]
            done.append(stack(solved))
            done_beside.append(stack(solved_beside))
            inverse_ref[first : first + 8, :] = done_beside[-1]
            if p + 1 < block // 8:
                twice = [weighted([inv[k, i] for k in range(i, 8)], solved[i:]) for i in range(8)]
                twice_beside = [weighted([inv[k, i] for k in range(i, 8)], solved_beside[i:]) for i in range(8)]
            for q in range(p + 1, block // 8):
                columns = [jnp.broadcast_to(here[q][:, first + j : first + j + 1], top.shape) for j in range(8)]
                here[q] = here[q] - weighted(columns, twice)
                here_beside[q] = here_beside[q] - weighted(columns, twice_beside)
        if start + block < size:
            solved = jnp.concatenate(done, axis=0)
            both = jnp.concatenate([solved, jnp.concatenate(done_beside, axis=0)], axis=1)
            taken = exact(solved.T[start + block :], both)
            schur = schur[block:] - taken[:, 0:size]
            beside = beside[block:] - taken[:, size:]
    inverse = inverse_ref[...]
    coarse = inverse.astype(BF16)
    rest = inverse - coarse.astype(F32)
    fine = rest.astype(BF16)
    finest = (rest - fine.astype(F32)).astype(BF16)
    own = own_ref[...]
    ortho_out[...] = nn(coarse, own) + (nn(fine, own) + nn(finest, own))
    half_solved = exact(inverse, total_ref[size : 2 * size, :] * scale)
    projected_out[...] = lax.dot_general(
        half_solved, inverse, (((1,), (1,)), ((), ())), precision=lax.Precision.HIGHEST, preferred_element_type=F32
    )


def finish(scale, total, own_part):
    states, nodes = own_part.shape
    return pl.pallas_call(
        lambda *refs: finish_body(scale, *refs),
        out_shape=(jax.ShapeDtypeStruct((states, nodes), F32), jax.ShapeDtypeStruct((states, states), F32)),
        in_specs=[spec()] * 2,
        out_specs=(spec(), spec()),
        scratch_shapes=[pltpu.VMEM((states, states), F32)],
        compiler_params=pltpu.CompilerParams(vmem_limit_bytes=16 * MIB),
        name="finish",
    )(total, own_part)


def shards(block, cell_nodes, send_lists, cell_matrix, cell_scale, potential):
    lists = send_lists[0]
    own, slots = block.shape[1], lists.shape[1]
    full = own + 2 * slots
    states_here = block.shape[0]
    states = 2 * states_here
    core, part = lax.axis_index("band"), lax.axis_index("dom")
    band = jnp.stack([core, part >= 2, part < lax.axis_size("dom") - 2]).astype(jnp.int32)
    potential = potential.reshape(1, own)

    to_left, to_right = send_first(block, lists)
    to_left, to_right, cell_nodes = lax.optimization_barrier((to_left, to_right, cell_nodes))
    from_left = shift(to_right, "dom", 1)
    from_right = shift(to_left, "dom", -1)
    mine = build(band, cell_nodes, cell_matrix, cell_scale, full)
    mine, from_left, from_right = lax.optimization_barrier((mine, from_left, from_right))
    other = lax.ppermute(mine, "band", [(0, 1), (1, 0)])
    x_here = jnp.concatenate([block, from_left[:states_here], from_right[:states_here]], axis=1)
    x0 = lax.all_gather(x_here, "band", axis=0, tiled=True)

    shapes = apply_shapes(states, own, slots)
    x_shape = jax.ShapeDtypeStruct((states, full), BF16)
    fixed = (band, mine, other, potential, lists)
    ends = fixed + (from_left, from_right)
    other_shape = jax.ShapeDtypeStruct(other.shape, other.dtype)
    other, partial, ghost, near, far = stage_call(
        first_body, fixed + (x0,), (other_shape,) + shapes, "apply_one", (pltpu.SemaphoreType.DMA,), (2,)
    )
    fixed = (band, mine, other, potential, lists)
    ends = fixed + (from_left, from_right)
    got = exchange(core, near, far)
    x1, partial, ghost, near, far = stage_call(
        lambda *r: next_body(False, *r), ends + (partial, ghost, got), (x_shape,) + shapes, "apply_two"
    )
    got = exchange(core, near, far)
    x2, partial, ghost, near, far = stage_call(
        lambda *r: next_body(True, *r), ends + (partial, ghost, got, x0), (x_shape,) + shapes, "apply_three"
    )
    got = exchange(core, near, far)
    own_part, sums = stage_call(
        last_body,
        ends + (partial, ghost, got, x1),
        (jax.ShapeDtypeStruct((states, own // 2), BF16), jax.ShapeDtypeStruct((2 * states, states), F32)),
        "apply_four",
        (pltpu.VMEM((states, full), BF16), pltpu.VMEM((1, own), F32)),
    )
    return finish(1.0 / (own * lax.axis_size("dom")), sum_everywhere(sums), own_part)


def solution(mesh):
    return jax.shard_map(
        shards,
        mesh=mesh,
        in_specs=(P("band", "dom"), P("dom", None), P("dom", None, None), P(), P("dom"), P("dom")),
        out_specs=(P(None, ("dom", "band")), P()),
        check_vma=False,
    )
```

```python
import jax
import jax.numpy as jnp
from jax import lax
from jax.experimental import pallas as pl
from jax.experimental.pallas import tpu as pltpu
from jax.sharding import PartitionSpec as P

BOTH = ("dom", "band")
BF16 = jnp.bfloat16
F32 = jnp.float32
CELL_PAD = 128
MIB = 1 << 20


def spec(space=pltpu.VMEM):
    return pl.BlockSpec(memory_space=space)


def nn(a, b):
    return lax.dot_general(a, b, (((1,), (0,)), ((), ())), preferred_element_type=F32)


def nt(a, b):
    return lax.dot_general(a, b, (((1,), (1,)), ((), ())), preferred_element_type=F32)


def one_hot(rows, row):
    hit = lax.broadcasted_iota(row.dtype, (rows, row.shape[1]), 0) == row
    return hit.astype(F32).astype(BF16)


def pair_mask(column, row):
    return (column == row).astype(F32).astype(BF16)


def send_body(block_ref, lists_ref, left_ref, right_ref):
    own = block_ref.shape[1]
    states = block_ref.shape[0]
    lists = lists_ref[...]
    slots = lists.shape[1]
    part = lax.broadcasted_iota(jnp.int32, (16, slots), 0)
    codes = jnp.zeros((16, slots), jnp.int32)
    for side in (0, 1):
        one = lists[side : side + 1]
        codes = jnp.where(part == 2 * side, one >> 5, codes)
        codes = jnp.where(part == 2 * side + 1, one & 31, codes)
    codes = codes.astype(F32).astype(BF16)
    for side, out in ((0, left_ref), (1, right_ref)):
        out[0:states, :] = nn(block_ref[...], one_hot(own, lists[side : side + 1])).astype(BF16)
        out[states : states + 16, :] = codes


def send_first(block, lists):
    states, slots = block.shape[0], lists.shape[1]
    shape = jax.ShapeDtypeStruct((states + 16, slots), BF16)
    return pl.pallas_call(
        send_body,
        out_shape=(shape, shape),
        in_specs=[spec()] * 2,
        out_specs=(spec(), spec()),
        name="send_first",
    )(block, lists)


def build_body(band_ref, packed_ref, out_ref, hot, left):
    half, full = out_ref.shape
    cells = left.shape[1] // CELL_PAD
    first = band_ref[0] * half
    matrix = packed_ref[cells : cells + CELL_PAD, :].T
    nothing = jnp.zeros((CELL_PAD, CELL_PAD), F32)
    pair_matrix = jnp.concatenate(
        [jnp.concatenate([matrix, nothing], axis=1), jnp.concatenate([nothing, matrix], axis=1)], axis=0
    ).astype(BF16)
    for pair in range(cells // 2):
        both = (2 * pair, 2 * pair + 1)
        row = jnp.concatenate([packed_ref[c : c + 1, :] for c in both], axis=1).astype(jnp.int32)
        at = cells + CELL_PAD
        gain = [jnp.broadcast_to(packed_ref[at : at + 1, c : c + 1], (1, CELL_PAD)) for c in both]
        cols = slice(pair * 2 * CELL_PAD, (pair + 1) * 2 * CELL_PAD)
        product = nn(one_hot(half, row - first), pair_matrix)
        left[:, cols] = (product * jnp.concatenate(gain, axis=1)).astype(BF16)
        hot[:, cols] = one_hot(full, row)
    for at in range(0, half, 256):
        out_ref[at : at + 256, :] = nt(left[at : at + 256, :], hot[...]).astype(BF16)


def build(band, cell_nodes, cell_matrix, cell_scale, full):
    cells, nodes = cell_nodes.shape
    half = full // 2
    entries = cells * CELL_PAD
    spare = CELL_PAD - nodes
    packed = jnp.concatenate(
        [
            jnp.pad(cell_nodes.astype(F32), ((0, 0), (0, spare)), constant_values=-8192.0),
            jnp.pad(cell_matrix.astype(F32), ((0, spare), (0, spare))),
            jnp.pad(cell_scale[None], ((0, 7), (0, CELL_PAD - cells))),
        ],
        axis=0,
    )
    return pl.pallas_call(
        build_body,
        out_shape=jax.ShapeDtypeStruct((half, full), BF16),
        in_specs=[spec(pltpu.SMEM), spec()],
        out_specs=spec(),
        scratch_shapes=[pltpu.VMEM((full, entries), BF16), pltpu.VMEM((half, entries), BF16)],
        compiler_params=pltpu.CompilerParams(vmem_limit_bytes=26 * MIB),
        cost_estimate=pl.CostEstimate(
            flops=2 * half * entries * full, bytes_accessed=2 * half * full, transcendentals=0
        ),
        name="build",
    )(band, packed)


def decode(codes_ref):
    slots = codes_ref.shape[1]
    codes = codes_ref[codes_ref.shape[0] - 16 :, :].astype(F32)
    rows = [codes[2 * s : 2 * s + 1] * 32.0 + codes[2 * s + 1 : 2 * s + 2] for s in (0, 1)]
    part = lax.broadcasted_iota(jnp.int32, (8, slots), 0)
    both = jnp.where(part == 0, rows[0], rows[1])
    columns = both.T
    return rows, [columns[:, 0:1], columns[:, 1:2]]


def assemble(band_ref, partial_ref, ghost_ref, got_ref, lists, from_left_ref, from_right_ref, own):
    slots = lists.shape[1]
    (left_rows, left_cols), (right_rows, right_cols) = decode(from_left_ref), decode(from_right_ref)
    ghost = ghost_ref[...]
    ghost_left, ghost_right = ghost[:, 0:slots], ghost[:, slots : 2 * slots]
    states = ghost.shape[0]
    got_left, got_right = got_ref[0:states, :], got_ref[states : 2 * states, :]
    near_left, near_right = got_left[:, 0:slots], got_right[:, 0:slots]
    gone_left, gone_right = ((1 - band_ref[1 + side]).astype(F32) * 4096.0 for side in (0, 1))
    whole_own = (
        partial_ref[...]
        + nt(near_left, one_hot(own, lists[0:1]))
        + nt(near_right, one_hot(own, lists[1:2]))
    )
    whole_left = (
        got_left[:, slots : 2 * slots].astype(F32)
        + nn(got_left[:, 2 * slots : 3 * slots], pair_mask(left_cols[0] + gone_left, left_rows[1]))
        + nn(ghost_left, pair_mask(left_cols[1], left_rows[1]))
    )
    whole_right = (
        got_right[:, slots : 2 * slots].astype(F32)
        + nn(got_right[:, 2 * slots : 3 * slots], pair_mask(right_cols[1] + gone_right, right_rows[0]))
        + nn(ghost_right, pair_mask(right_cols[0], right_rows[0]))
    )
    return whole_own, whole_left, whole_right


def times_half(which, x_ref, w_ref, cols):
    half = w_ref.shape[0]
    return nn(x_ref[:, pl.ds(pl.multiple_of(which * half, 128), half)], w_ref[:, cols])


def times_operator(band, x_ref, mine_ref, other_ref, cols):
    return times_half(band, x_ref, mine_ref, cols) + times_half(1 - band, x_ref, other_ref, cols)


def apply_body(band_ref, x_ref, mine_ref, other_ref, *refs):
    give(band_ref, times_operator(band_ref[0], x_ref, mine_ref, other_ref, slice(None)), x_ref, *refs)


def give(band_ref, result, x_ref, potential_ref, lists, partial_out, ghost_out, near_out, far_out):
    own = partial_out.shape[1]
    slots = lists.shape[1]
    partial = result[:, 0:own] + potential_ref[...] * x_ref[:, 0:own].astype(F32)
    partial_out[...] = partial
    ghost = result[:, own:].astype(BF16)
    ghost_out[...] = ghost
    right = band_ref[0] == 1
    mine = jnp.where(right, lists[1:2], lists[0:1])
    edge = jnp.where(right, ghost[:, slots : 2 * slots], ghost[:, 0:slots])
    near_out[:, 0:slots] = edge
    near_out[:, slots : 2 * slots] = nn(partial.astype(BF16), one_hot(own, mine)).astype(BF16)
    far_out[...] = edge


def first_body(
    band_ref, mine_ref, other_hbm, potential_ref, lists_ref, x_ref, other_out, partial_out, ghost_out, near_out,
    far_out, sem,
):
    piece = other_out.shape[0] // 4
    arrivals = [
        pltpu.make_async_copy(other_hbm.at[i * piece : (i + 1) * piece], other_out.at[i * piece : (i + 1) * piece], sem.at[i])
        for i in range(4)
    ]
    for arrival in arrivals:
        arrival.start()
    result = times_half(band_ref[0], x_ref, mine_ref, slice(None))
    for arrival in arrivals:
        arrival.wait()
    result = result + times_half(1 - band_ref[0], x_ref, other_out, slice(None))
    give(band_ref, result, x_ref, potential_ref, lists_ref[...], partial_out, ghost_out, near_out, far_out)


def new_states(older_ref, x_out, pieces):
    own = pieces[0].shape[1]
    slots = pieces[1].shape[1]
    at = 0
    for piece in pieces:
        cols = slice(at, at + piece.shape[1])
        if older_ref is not None:
            piece = 2.0 * piece - older_ref[:, cols].astype(F32)
        x_out[:, cols] = piece.astype(BF16)
        at += piece.shape[1]


def next_body(chebyshev, *refs):
    band_ref, mine_ref, other_ref, potential_ref, lists_ref, fl_ref, fr_ref, partial_ref, ghost_ref, got_ref = refs[:10]
    older_ref = refs[10] if chebyshev else None
    x_out, *outs = refs[11:] if chebyshev else refs[10:]
    lists = lists_ref[...]
    own = partial_ref.shape[1]
    new_states(older_ref, x_out, assemble(band_ref, partial_ref, ghost_ref, got_ref, lists, fl_ref, fr_ref, own))
    apply_body(band_ref, x_out, mine_ref, other_ref, potential_ref, lists, *outs)


def last_body(
    band_ref, mine_ref, other_ref, potential_ref, lists_ref, fl_ref, fr_ref, partial_ref, ghost_ref, got_ref,
    older_ref, own_out, sums_out, x_all, pot,
):
    lists = lists_ref[...]
    own = partial_ref.shape[1]
    states = partial_ref.shape[0]
    slots = lists.shape[1]
    new_states(older_ref, x_all, assemble(band_ref, partial_ref, ghost_ref, got_ref, lists, fl_ref, fr_ref, own))
    pot[...] = potential_ref[...]
    half = own // 2
    mine = pl.ds(pl.multiple_of(band_ref[0] * half, 128), half)
    edge = pl.ds(pl.multiple_of(own + band_ref[0] * slots, 128), slots)
    x_mine = x_all[:, mine]
    own_out[...] = x_mine
    sums_out[0:states, :] = nt(x_mine, x_mine)
    image = times_operator(band_ref[0], x_all, mine_ref, other_ref, mine) + pot[:, mine] * x_mine.astype(F32)
    image_edge = times_operator(band_ref[0], x_all, mine_ref, other_ref, edge)
    sums_out[states : 2 * states, :] = nt(x_mine, image.astype(BF16)) + nt(x_all[:, edge], image_edge.astype(BF16))


def apply_shapes(states, own, slots):
    return (
        jax.ShapeDtypeStruct((states, own), F32),
        jax.ShapeDtypeStruct((states, 2 * slots), BF16),
        jax.ShapeDtypeStruct((states, 2 * slots), BF16),
        jax.ShapeDtypeStruct((states, slots), BF16),
    )


def stage_call(body, args, shapes, name, scratch=(), anywhere=()):
    return pl.pallas_call(
        body,
        out_shape=tuple(shapes),
        in_specs=[spec(pltpu.SMEM)] + [spec(pl.ANY if i in anywhere else pltpu.VMEM) for i in range(1, len(args))],
        out_specs=tuple(spec() for _ in shapes),
        scratch_shapes=list(scratch),
        compiler_params=pltpu.CompilerParams(vmem_limit_bytes=16 * MIB),
        name=name,
    )(*args)


def shift(x, axis, by):
    devices = lax.axis_size(axis)
    return lax.ppermute(x, axis, [(i, i + by) for i in range(devices) if 0 <= i + by < devices])


def across(x, by):
    parts = lax.axis_size("dom")
    pairs = [(2 * d + 1, 2 * (d + by)) for d in range(parts - by)]
    pairs += [(2 * (d + by), 2 * d + 1) for d in range(parts - by)]
    return lax.ppermute(x, BOTH, pairs)


def far_groups(parts):
    pairs = [[2 * d + 1, 2 * d + 4] for d in range(parts - 2)]
    return pairs + [[0, 2], [2 * parts - 3, 2 * parts - 1]]


def exchange(band, near, far):
    rows = far.shape[0]
    near = across(near, 1)
    both = lax.all_gather(far, BOTH, axis_index_groups=far_groups(lax.axis_size("dom")), axis=0, tiled=True)
    far = lax.dynamic_slice_in_dim(both, band * rows, rows, 0)
    return lax.all_gather(jnp.concatenate([near, far], axis=1), "band", axis=0, tiled=True)


def group_lists():
    planes, along_z = {}, {}
    for x in range(4):
        for z in range(16):
            for y in range(4):
                for b in range(2):
                    i = ((x * 16 + z) * 4 + y) * 2 + b
                    planes.setdefault(z, []).append(i)
                    along_z.setdefault((x, y, b), []).append(i)
    return list(planes.values()), list(along_z.values())


def swap_pieces(x, groups):
    return lax.all_to_all(x, BOTH, 0, 0, axis_index_groups=groups, tiled=True)


def copies(piece, count):
    return jnp.broadcast_to(piece[None], (count,) + piece.shape).reshape(count * piece.shape[0], piece.shape[1])


def sum_pieces(x, count):
    return x.reshape(count, x.shape[0] // count, x.shape[1]).sum(0)


def sum_everywhere(x):
    planes, along_z = group_lists()
    in_plane, depth = len(planes[0]), len(along_z[0])
    piece = sum_pieces(swap_pieces(x, planes), in_plane)
    piece = sum_pieces(swap_pieces(copies(piece, depth), along_z), depth)
    return swap_pieces(copies(piece, in_plane), planes)


def exact(a, b):
    return jnp.dot(a, b, precision=lax.Precision.HIGHEST, preferred_element_type=F32)


def weighted(weights, rows):
    total = None
    for w, r in zip(weights, rows):
        total = w * r if total is None else total + w * r
    return total


def stack(rows):
    part = lax.broadcasted_iota(jnp.int32, rows[0].shape, 0)
    out = rows[0]
    for i in range(1, len(rows)):
        out = jnp.where(part == i, rows[i], out)
    return out


def inverse_of_eight(panel, first):
    wide = panel.shape
    columns = [jnp.broadcast_to(panel[:, first + j : first + j + 1], wide) for j in range(8)]
    low = {(i, j): jnp.broadcast_to(columns[j][i : i + 1, :], wide) for j in range(8) for i in range(j, 8)}
    inv = {}
    for j in range(8):
        inv[j, j] = lax.rsqrt(low[j, j])
        for i in range(j + 1, 8):
            low[i, j] = low[i, j] * inv[j, j]
        for k in range(j + 1, 8):
            for i in range(k, 8):
                low[i, k] = low[i, k] - low[i, j] * low[k, j]
        for k in range(j):
            inv[j, k] = -inv[j, j] * weighted([low[j, m] for m in range(k, j)], [inv[m, k] for m in range(k, j)])
    return inv


def finish_body(scale, total_ref, own_ref, ortho_out, projected_out, inverse_ref):
    size = total_ref.shape[1]
    block = 32
    schur = total_ref[0:size, :] * scale
    at = lax.broadcasted_iota(jnp.int32, (size, size), 0)
    beside = (at == lax.broadcasted_iota(jnp.int32, (size, size), 1)).astype(F32)
    for start in range(0, size, block):
        here = [schur[i : i + 8] for i in range(0, block, 8)]
        here_beside = [beside[i : i + 8] for i in range(0, block, 8)]
        done, done_beside = [], []
        for p in range(block // 8):
            first = start + 8 * p
            top, top_beside = here[p], here_beside[p]
            inv = inverse_of_eight(top, first)
            rows = [jnp.broadcast_to(top[i : i + 1], top.shape) for i in range(8)]
            rows_beside = [jnp.broadcast_to(top_beside[i : i + 1], top.shape) for i in range(8)]
            solved = [weighted([inv[i, k] for k in range(i + 1)], rows) for i in range(8)]
            solved_beside = [weighted([inv[i, k] for k in range(i + 1)], rows_beside) for i in range(8)]
            done.append(stack(solved))
            done_beside.append(stack(solved_beside))
            inverse_ref[first : first + 8, :] = done_beside[-1]
            if p + 1 < block // 8:
                twice = [weighted([inv[k, i] for k in range(i, 8)], solved[i:]) for i in range(8)]
                twice_beside = [weighted([inv[k, i] for k in range(i, 8)], solved_beside[i:]) for i in range(8)]
            for q in range(p + 1, block // 8):
                columns = [jnp.broadcast_to(here[q][:, first + j : first + j + 1], top.shape) for j in range(8)]
                here[q] = here[q] - weighted(columns, twice)
                here_beside[q] = here_beside[q] - weighted(columns, twice_beside)
        if start + block < size:
            solved = jnp.concatenate(done, axis=0)
            both = jnp.concatenate([solved, jnp.concatenate(done_beside, axis=0)], axis=1)
            taken = exact(solved.T[start + block :], both)
            schur = schur[block:] - taken[:, 0:size]
            beside = beside[block:] - taken[:, size:]
    inverse = inverse_ref[...]
    coarse = inverse.astype(BF16)
    rest = inverse - coarse.astype(F32)
    fine = rest.astype(BF16)
    finest = (rest - fine.astype(F32)).astype(BF16)
    own = own_ref[...]
    ortho_out[...] = nn(coarse, own) + (nn(fine, own) + nn(finest, own))
    half_solved = exact(inverse, total_ref[size : 2 * size, :] * scale)
    projected_out[...] = lax.dot_general(
        half_solved, inverse, (((1,), (1,)), ((), ())), precision=lax.Precision.HIGHEST, preferred_element_type=F32
    )


def finish(scale, total, own_part):
    states, nodes = own_part.shape
    return pl.pallas_call(
        lambda *refs: finish_body(scale, *refs),
        out_shape=(jax.ShapeDtypeStruct((states, nodes), F32), jax.ShapeDtypeStruct((states, states), F32)),
        in_specs=[spec()] * 2,
        out_specs=(spec(), spec()),
        scratch_shapes=[pltpu.VMEM((states, states), F32)],
        compiler_params=pltpu.CompilerParams(vmem_limit_bytes=16 * MIB),
        name="finish",
    )(total, own_part)


def shards(block, cell_nodes, send_lists, cell_matrix, cell_scale, potential):
    lists = send_lists[0]
    own, slots = block.shape[1], lists.shape[1]
    full = own + 2 * slots
    states_here = block.shape[0]
    states = 2 * states_here
    core, part = lax.axis_index("band"), lax.axis_index("dom")
    band = jnp.stack([core, part >= 2, part < lax.axis_size("dom") - 2]).astype(jnp.int32)
    potential = potential.reshape(1, own)

    to_left, to_right = send_first(block, lists)
    to_left, to_right, cell_nodes = lax.optimization_barrier((to_left, to_right, cell_nodes))
    from_left = shift(to_right, "dom", 1)
    from_right = shift(to_left, "dom", -1)
    mine = build(band, cell_nodes, cell_matrix, cell_scale, full)
    mine, from_left, from_right = lax.optimization_barrier((mine, from_left, from_right))
    other = lax.ppermute(mine, "band", [(0, 1), (1, 0)])
    x_here = jnp.concatenate([block, from_left[:states_here], from_right[:states_here]], axis=1)
    x0 = lax.all_gather(x_here, "band", axis=0, tiled=True)

    shapes = apply_shapes(states, own, slots)
    x_shape = jax.ShapeDtypeStruct((states, full), BF16)
    fixed = (band, mine, other, potential, lists)
    ends = fixed + (from_left, from_right)
    other_shape = jax.ShapeDtypeStruct(other.shape, other.dtype)
    other, partial, ghost, near, far = stage_call(
        first_body, fixed + (x0,), (other_shape,) + shapes, "apply_one", (pltpu.SemaphoreType.DMA((4,)),), (2,)
    )
    fixed = (band, mine, other, potential, lists)
    ends = fixed + (from_left, from_right)
    got = exchange(core, near, far)
    x1, partial, ghost, near, far = stage_call(
        lambda *r: next_body(False, *r), ends + (partial, ghost, got), (x_shape,) + shapes, "apply_two"
    )
    got = exchange(core, near, far)
    x2, partial, ghost, near, far = stage_call(
        lambda *r: next_body(True, *r), ends + (partial, ghost, got, x0), (x_shape,) + shapes, "apply_three"
    )
    got = exchange(core, near, far)
    own_part, sums = stage_call(
        last_body,
        ends + (partial, ghost, got, x1),
        (jax.ShapeDtypeStruct((states, own // 2), BF16), jax.ShapeDtypeStruct((2 * states, states), F32)),
        "apply_four",
        (pltpu.VMEM((states, full), BF16), pltpu.VMEM((1, own), F32)),
    )
    return finish(1.0 / (own * lax.axis_size("dom")), sum_everywhere(sums), own_part)


def solution(mesh):
    return jax.shard_map(
        shards,
        mesh=mesh,
        in_specs=(P("band", "dom"), P("dom", None), P("dom", None, None), P(), P("dom"), P("dom")),
        out_specs=(P(None, ("dom", "band")), P()),
        check_vma=False,
    )
```

```python
import jax
import jax.numpy as jnp
from jax import lax
from jax.experimental import pallas as pl
from jax.experimental.pallas import tpu as pltpu
from jax.sharding import PartitionSpec as P

BOTH = ("dom", "band")
BF16 = jnp.bfloat16
F32 = jnp.float32
CELL_PAD = 128
MIB = 1 << 20


def spec(space=pltpu.VMEM):
    return pl.BlockSpec(memory_space=space)


def nn(a, b):
    return lax.dot_general(a, b, (((1,), (0,)), ((), ())), preferred_element_type=F32)


def nt(a, b):
    return lax.dot_general(a, b, (((1,), (1,)), ((), ())), preferred_element_type=F32)


def one_hot(rows, row):
    hit = lax.broadcasted_iota(row.dtype, (rows, row.shape[1]), 0) == row
    return hit.astype(F32).astype(BF16)


def pair_mask(column, row):
    return (column == row).astype(F32).astype(BF16)


def send_body(parts, part_ref, block_ref, lists_ref, left_ref, right_ref):
    own = block_ref.shape[1]
    states = block_ref.shape[0]
    lists = lists_ref[...]
    slots = lists.shape[1]
    part = lax.broadcasted_iota(jnp.int32, (16, slots), 0)
    codes = jnp.where(part == 4, 1, 0)
    for side, end in ((0, 0), (1, parts - 1)):
        one = lists[side : side + 1]
        codes = jnp.where(part == 2 * side, (one >> 5) + jnp.where(part_ref[0] == end, 128, 0), codes)
        codes = jnp.where(part == 2 * side + 1, one & 31, codes)
    codes = codes.astype(F32).astype(BF16)
    for side, out in ((0, left_ref), (1, right_ref)):
        out[0:states, :] = nn(block_ref[...], one_hot(own, lists[side : side + 1])).astype(BF16)
        out[states : states + 16, :] = codes


def send_first(parts, part, block, lists):
    states, slots = block.shape[0], lists.shape[1]
    shape = jax.ShapeDtypeStruct((states + 16, slots), BF16)
    return pl.pallas_call(
        lambda *refs: send_body(parts, *refs),
        out_shape=(shape, shape),
        in_specs=[spec(pltpu.SMEM)] + [spec()] * 2,
        out_specs=(spec(), spec()),
        name="send_first",
    )(part, block, lists)


def build_body(band_ref, packed_ref, out_ref, hot, left):
    half, full = out_ref.shape
    cells = left.shape[1] // CELL_PAD
    first = band_ref[0] * half
    matrix = packed_ref[cells : cells + CELL_PAD, :].T
    nothing = jnp.zeros((CELL_PAD, CELL_PAD), F32)
    pair_matrix = jnp.concatenate(
        [jnp.concatenate([matrix, nothing], axis=1), jnp.concatenate([nothing, matrix], axis=1)], axis=0
    ).astype(BF16)
    for pair in range(cells // 2):
        both = (2 * pair, 2 * pair + 1)
        row = jnp.concatenate([packed_ref[c : c + 1, :] for c in both], axis=1).astype(jnp.int32)
        at = cells + CELL_PAD
        gain = [jnp.broadcast_to(packed_ref[at : at + 1, c : c + 1], (1, CELL_PAD)) for c in both]
        cols = slice(pair * 2 * CELL_PAD, (pair + 1) * 2 * CELL_PAD)
        product = nn(one_hot(half, row - first), pair_matrix)
        left[:, cols] = (product * jnp.concatenate(gain, axis=1)).astype(BF16)
        hot[:, cols] = one_hot(full, row)
    for at in range(0, half, 256):
        out_ref[at : at + 256, :] = nt(left[at : at + 256, :], hot[...]).astype(BF16)


def build(band, cell_nodes, cell_matrix, cell_scale, full):
    cells, nodes = cell_nodes.shape
    half = full // 2
    entries = cells * CELL_PAD
    spare = CELL_PAD - nodes
    packed = jnp.concatenate(
        [
            jnp.pad(cell_nodes.astype(F32), ((0, 0), (0, spare)), constant_values=-8192.0),
            jnp.pad(cell_matrix.astype(F32), ((0, spare), (0, spare))),
            jnp.pad(cell_scale[None], ((0, 7), (0, CELL_PAD - cells))),
        ],
        axis=0,
    )
    return pl.pallas_call(
        build_body,
        out_shape=jax.ShapeDtypeStruct((half, full), BF16),
        in_specs=[spec(pltpu.SMEM), spec()],
        out_specs=spec(),
        scratch_shapes=[pltpu.VMEM((full, entries), BF16), pltpu.VMEM((half, entries), BF16)],
        compiler_params=pltpu.CompilerParams(vmem_limit_bytes=26 * MIB),
        cost_estimate=pl.CostEstimate(
            flops=2 * half * entries * full, bytes_accessed=2 * half * full, transcendentals=0
        ),
        name="build",
    )(band, packed)


def decode(codes_ref):
    slots = codes_ref.shape[1]
    codes = codes_ref[codes_ref.shape[0] - 16 :, :].astype(F32)
    rows = [codes[2 * s : 2 * s + 1] * 32.0 + codes[2 * s + 1 : 2 * s + 2] for s in (0, 1)]
    part = lax.broadcasted_iota(jnp.int32, (8, slots), 0)
    both = jnp.where(part == 0, rows[0], rows[1])
    columns = both.T + (1.0 - codes[4:5, 0:1]) * 16384.0
    return rows, [columns[:, 0:1], columns[:, 1:2]]


def assemble(partial_ref, ghost_ref, got_ref, lists, from_left_ref, from_right_ref, own):
    slots = lists.shape[1]
    (left_rows, left_cols), (right_rows, right_cols) = decode(from_left_ref), decode(from_right_ref)
    ghost = ghost_ref[...]
    ghost_left, ghost_right = ghost[:, 0:slots], ghost[:, slots : 2 * slots]
    states = ghost.shape[0]
    got_left, got_right = got_ref[0:states, :], got_ref[states : 2 * states, :]
    near_left, near_right = got_left[:, 0:slots], got_right[:, 0:slots]
    whole_own = (
        partial_ref[...]
        + nt(near_left, one_hot(own, lists[0:1]))
        + nt(near_right, one_hot(own, lists[1:2]))
    )
    whole_left = (
        got_left[:, slots : 2 * slots].astype(F32)
        + nn(got_left[:, 2 * slots : 3 * slots], pair_mask(left_cols[0], left_rows[1]))
        + nn(ghost_left, pair_mask(left_cols[1], left_rows[1]))
    )
    whole_right = (
        got_right[:, slots : 2 * slots].astype(F32)
        + nn(got_right[:, 2 * slots : 3 * slots], pair_mask(right_cols[1], right_rows[0]))
        + nn(ghost_right, pair_mask(right_cols[0], right_rows[0]))
    )
    return whole_own, whole_left, whole_right


def times_half(which, x_ref, w_ref, cols):
    half = w_ref.shape[0]
    return nn(x_ref[:, pl.ds(pl.multiple_of(which * half, 128), half)], w_ref[:, cols])


def times_operator(band, x_ref, mine_ref, other_ref, cols):
    return times_half(band, x_ref, mine_ref, cols) + times_half(1 - band, x_ref, other_ref, cols)


def apply_body(band_ref, x_ref, mine_ref, other_ref, *refs):
    give(band_ref, times_operator(band_ref[0], x_ref, mine_ref, other_ref, slice(None)), x_ref, *refs)


def give(band_ref, result, x_ref, potential_ref, lists, partial_out, ghost_out, near_out, far_out):
    own = partial_out.shape[1]
    slots = lists.shape[1]
    partial = result[:, 0:own] + potential_ref[...] * x_ref[:, 0:own].astype(F32)
    partial_out[...] = partial
    ghost = result[:, own:].astype(BF16)
    ghost_out[...] = ghost
    right = band_ref[0] == 1
    mine = jnp.where(right, lists[1:2], lists[0:1])
    edge = jnp.where(right, ghost[:, slots : 2 * slots], ghost[:, 0:slots])
    near_out[:, 0:slots] = edge
    near_out[:, slots : 2 * slots] = nn(partial.astype(BF16), one_hot(own, mine)).astype(BF16)
    far_out[...] = edge


def first_body(
    band_ref, mine_ref, other_hbm, potential_ref, lists_ref, x_ref, other_out, partial_out, ghost_out, near_out,
    far_out, sem,
):
    piece = other_out.shape[0] // 4
    arrivals = [
        pltpu.make_async_copy(other_hbm.at[i * piece : (i + 1) * piece], other_out.at[i * piece : (i + 1) * piece], sem.at[i])
        for i in range(4)
    ]
    for arrival in arrivals:
        arrival.start()
    result = times_half(band_ref[0], x_ref, mine_ref, slice(None))
    for arrival in arrivals:
        arrival.wait()
    result = result + times_half(1 - band_ref[0], x_ref, other_out, slice(None))
    give(band_ref, result, x_ref, potential_ref, lists_ref[...], partial_out, ghost_out, near_out, far_out)


def new_states(older_ref, x_out, pieces):
    own = pieces[0].shape[1]
    slots = pieces[1].shape[1]
    at = 0
    for piece in pieces:
        cols = slice(at, at + piece.shape[1])
        if older_ref is not None:
            piece = 2.0 * piece - older_ref[:, cols].astype(F32)
        x_out[:, cols] = piece.astype(BF16)
        at += piece.shape[1]


def next_body(chebyshev, *refs):
    band_ref, mine_ref, other_ref, potential_ref, lists_ref, fl_ref, fr_ref, partial_ref, ghost_ref, got_ref = refs[:10]
    older_ref = refs[10] if chebyshev else None
    x_out, *outs = refs[11:] if chebyshev else refs[10:]
    lists = lists_ref[...]
    own = partial_ref.shape[1]
    new_states(older_ref, x_out, assemble(partial_ref, ghost_ref, got_ref, lists, fl_ref, fr_ref, own))
    apply_body(band_ref, x_out, mine_ref, other_ref, potential_ref, lists, *outs)


def last_body(
    band_ref, mine_ref, other_ref, potential_ref, lists_ref, fl_ref, fr_ref, partial_ref, ghost_ref, got_ref,
    older_ref, own_out, sums_out, x_all, pot,
):
    lists = lists_ref[...]
    own = partial_ref.shape[1]
    states = partial_ref.shape[0]
    slots = lists.shape[1]
    new_states(older_ref, x_all, assemble(partial_ref, ghost_ref, got_ref, lists, fl_ref, fr_ref, own))
    pot[...] = potential_ref[...]
    half = own // 2
    mine = pl.ds(pl.multiple_of(band_ref[0] * half, 128), half)
    edge = pl.ds(pl.multiple_of(own + band_ref[0] * slots, 128), slots)
    x_mine = x_all[:, mine]
    own_out[...] = x_mine
    sums_out[0:states, :] = nt(x_mine, x_mine)
    image = times_operator(band_ref[0], x_all, mine_ref, other_ref, mine) + pot[:, mine] * x_mine.astype(F32)
    image_edge = times_operator(band_ref[0], x_all, mine_ref, other_ref, edge)
    sums_out[states : 2 * states, :] = nt(x_mine, image.astype(BF16)) + nt(x_all[:, edge], image_edge.astype(BF16))


def apply_shapes(states, own, slots):
    return (
        jax.ShapeDtypeStruct((states, own), F32),
        jax.ShapeDtypeStruct((states, 2 * slots), BF16),
        jax.ShapeDtypeStruct((states, 2 * slots), BF16),
        jax.ShapeDtypeStruct((states, slots), BF16),
    )


def stage_call(body, args, shapes, name, scratch=(), anywhere=()):
    return pl.pallas_call(
        body,
        out_shape=tuple(shapes),
        in_specs=[spec(pltpu.SMEM)] + [spec(pl.ANY if i in anywhere else pltpu.VMEM) for i in range(1, len(args))],
        out_specs=tuple(spec() for _ in shapes),
        scratch_shapes=list(scratch),
        compiler_params=pltpu.CompilerParams(vmem_limit_bytes=16 * MIB),
        name=name,
    )(*args)


def shift(x, axis, by):
    devices = lax.axis_size(axis)
    return lax.ppermute(x, axis, [(i, i + by) for i in range(devices) if 0 <= i + by < devices])


def across(x, by):
    parts = lax.axis_size("dom")
    pairs = [(2 * d + 1, 2 * (d + by)) for d in range(parts - by)]
    pairs += [(2 * (d + by), 2 * d + 1) for d in range(parts - by)]
    return lax.ppermute(x, BOTH, pairs)


def far_groups(parts):
    pairs = [[2 * d + 1, 2 * d + 4] for d in range(parts - 2)]
    return pairs + [[0, 2], [2 * parts - 3, 2 * parts - 1]]


def exchange(band, near, far):
    rows = far.shape[0]
    near = across(near, 1)
    both = lax.all_gather(far, BOTH, axis_index_groups=far_groups(lax.axis_size("dom")), axis=0, tiled=True)
    far = lax.dynamic_slice_in_dim(both, band * rows, rows, 0)
    return lax.all_gather(jnp.concatenate([near, far], axis=1), "band", axis=0, tiled=True)


def group_lists():
    planes, along_z = {}, {}
    for x in range(4):
        for z in range(16):
            for y in range(4):
                for b in range(2):
                    i = ((x * 16 + z) * 4 + y) * 2 + b
                    planes.setdefault(z, []).append(i)
                    along_z.setdefault((x, y, b), []).append(i)
    return list(planes.values()), list(along_z.values())


def swap_pieces(x, groups):
    return lax.all_to_all(x, BOTH, 0, 0, axis_index_groups=groups, tiled=True)


def copies(piece, count):
    return jnp.broadcast_to(piece[None], (count,) + piece.shape).reshape(count * piece.shape[0], piece.shape[1])


def sum_pieces(x, count):
    return x.reshape(count, x.shape[0] // count, x.shape[1]).sum(0)


def sum_everywhere(x):
    planes, along_z = group_lists()
    in_plane, depth = len(planes[0]), len(along_z[0])
    piece = sum_pieces(swap_pieces(x, planes), in_plane)
    piece = sum_pieces(swap_pieces(copies(piece, depth), along_z), depth)
    return swap_pieces(copies(piece, in_plane), planes)


def exact(a, b):
    return jnp.dot(a, b, precision=lax.Precision.HIGHEST, preferred_element_type=F32)


def weighted(weights, rows):
    total = None
    for w, r in zip(weights, rows):
        total = w * r if total is None else total + w * r
    return total


def stack(rows):
    part = lax.broadcasted_iota(jnp.int32, rows[0].shape, 0)
    out = rows[0]
    for i in range(1, len(rows)):
        out = jnp.where(part == i, rows[i], out)
    return out


def inverse_of_eight(panel, first):
    wide = panel.shape
    columns = [jnp.broadcast_to(panel[:, first + j : first + j + 1], wide) for j in range(8)]
    low = {(i, j): jnp.broadcast_to(columns[j][i : i + 1, :], wide) for j in range(8) for i in range(j, 8)}
    inv = {}
    for j in range(8):
        inv[j, j] = lax.rsqrt(low[j, j])
        for i in range(j + 1, 8):
            low[i, j] = low[i, j] * inv[j, j]
        for k in range(j + 1, 8):
            for i in range(k, 8):
                low[i, k] = low[i, k] - low[i, j] * low[k, j]
        for k in range(j):
            inv[j, k] = -inv[j, j] * weighted([low[j, m] for m in range(k, j)], [inv[m, k] for m in range(k, j)])
    return inv


def finish_body(scale, total_ref, own_ref, ortho_out, projected_out, inverse_ref):
    size = total_ref.shape[1]
    block = 32
    schur = total_ref[0:size, :] * scale
    at = lax.broadcasted_iota(jnp.int32, (size, size), 0)
    beside = (at == lax.broadcasted_iota(jnp.int32, (size, size), 1)).astype(F32)
    for start in range(0, size, block):
        here = [schur[i : i + 8] for i in range(0, block, 8)]
        here_beside = [beside[i : i + 8] for i in range(0, block, 8)]
        done, done_beside = [], []
        for p in range(block // 8):
            first = start + 8 * p
            top, top_beside = here[p], here_beside[p]
            inv = inverse_of_eight(top, first)
            rows = [jnp.broadcast_to(top[i : i + 1], top.shape) for i in range(8)]
            rows_beside = [jnp.broadcast_to(top_beside[i : i + 1], top.shape) for i in range(8)]
            solved = [weighted([inv[i, k] for k in range(i + 1)], rows) for i in range(8)]
            solved_beside = [weighted([inv[i, k] for k in range(i + 1)], rows_beside) for i in range(8)]
            done.append(stack(solved))
            done_beside.append(stack(solved_beside))
            inverse_ref[first : first + 8, :] = done_beside[-1]
            if p + 1 < block // 8:
                twice = [weighted([inv[k, i] for k in range(i, 8)], solved[i:]) for i in range(8)]
                twice_beside = [weighted([inv[k, i] for k in range(i, 8)], solved_beside[i:]) for i in range(8)]
            for q in range(p + 1, block // 8):
                columns = [jnp.broadcast_to(here[q][:, first + j : first + j + 1], top.shape) for j in range(8)]
                here[q] = here[q] - weighted(columns, twice)
                here_beside[q] = here_beside[q] - weighted(columns, twice_beside)
        if start + block < size:
            solved = jnp.concatenate(done, axis=0)
            both = jnp.concatenate([solved, jnp.concatenate(done_beside, axis=0)], axis=1)
            taken = exact(solved.T[start + block :], both)
            schur = schur[block:] - taken[:, 0:size]
            beside = beside[block:] - taken[:, size:]
    inverse = inverse_ref[...]
    coarse = inverse.astype(BF16)
    rest = inverse - coarse.astype(F32)
    fine = rest.astype(BF16)
    finest = (rest - fine.astype(F32)).astype(BF16)
    own = own_ref[...]
    ortho_out[...] = nn(coarse, own) + (nn(fine, own) + nn(finest, own))
    half_solved = exact(inverse, total_ref[size : 2 * size, :] * scale)
    projected_out[...] = lax.dot_general(
        half_solved, inverse, (((1,), (1,)), ((), ())), precision=lax.Precision.HIGHEST, preferred_element_type=F32
    )


def finish(scale, total, own_part):
    states, nodes = own_part.shape
    return pl.pallas_call(
        lambda *refs: finish_body(scale, *refs),
        out_shape=(jax.ShapeDtypeStruct((states, nodes), F32), jax.ShapeDtypeStruct((states, states), F32)),
        in_specs=[spec()] * 2,
        out_specs=(spec(), spec()),
        scratch_shapes=[pltpu.VMEM((states, states), F32)],
        compiler_params=pltpu.CompilerParams(vmem_limit_bytes=16 * MIB),
        name="finish",
    )(total, own_part)


def shards(block, cell_nodes, send_lists, cell_matrix, cell_scale, potential):
    lists = send_lists[0]
    own, slots = block.shape[1], lists.shape[1]
    full = own + 2 * slots
    states_here = block.shape[0]
    states = 2 * states_here
    core = lax.axis_index("band")
    band = core.astype(jnp.int32).reshape(1)
    part = lax.axis_index("dom").astype(jnp.int32).reshape(1)
    potential = potential.reshape(1, own)

    to_left, to_right = send_first(lax.axis_size("dom"), part, block, lists)
    to_left, to_right, cell_nodes = lax.optimization_barrier((to_left, to_right, cell_nodes))
    from_left = shift(to_right, "dom", 1)
    from_right = shift(to_left, "dom", -1)
    mine = build(band, cell_nodes, cell_matrix, cell_scale, full)
    mine, from_left, from_right = lax.optimization_barrier((mine, from_left, from_right))
    other = lax.ppermute(mine, "band", [(0, 1), (1, 0)])
    x_here = jnp.concatenate([block, from_left[:states_here], from_right[:states_here]], axis=1)
    x0 = lax.all_gather(x_here, "band", axis=0, tiled=True)

    shapes = apply_shapes(states, own, slots)
    x_shape = jax.ShapeDtypeStruct((states, full), BF16)
    fixed = (band, mine, other, potential, lists)
    ends = fixed + (from_left, from_right)
    other_shape = jax.ShapeDtypeStruct(other.shape, other.dtype)
    other, partial, ghost, near, far = stage_call(
        first_body, fixed + (x0,), (other_shape,) + shapes, "apply_one", (pltpu.SemaphoreType.DMA((4,)),), (2,)
    )
    fixed = (band, mine, other, potential, lists)
    ends = fixed + (from_left, from_right)
    got = exchange(core, near, far)
    x1, partial, ghost, near, far = stage_call(
        lambda *r: next_body(False, *r), ends + (partial, ghost, got), (x_shape,) + shapes, "apply_two"
    )
    got = exchange(core, near, far)
    x2, partial, ghost, near, far = stage_call(
        lambda *r: next_body(True, *r), ends + (partial, ghost, got, x0), (x_shape,) + shapes, "apply_three"
    )
    got = exchange(core, near, far)
    own_part, sums = stage_call(
        last_body,
        ends + (partial, ghost, got, x1),
        (jax.ShapeDtypeStruct((states, own // 2), BF16), jax.ShapeDtypeStruct((2 * states, states), F32)),
        "apply_four",
        (pltpu.VMEM((states, full), BF16), pltpu.VMEM((1, own), F32)),
    )
    return finish(1.0 / (own * lax.axis_size("dom")), sum_everywhere(sums), own_part)


def solution(mesh):
    return jax.shard_map(
        shards,
        mesh=mesh,
        in_specs=(P("band", "dom"), P("dom", None), P("dom", None, None), P(), P("dom"), P("dom")),
        out_specs=(P(None, ("dom", "band")), P()),
        check_vma=False,
    )
```

```python
import jax
import jax.numpy as jnp
from jax import lax
from jax.experimental import pallas as pl
from jax.experimental.pallas import tpu as pltpu
from jax.sharding import PartitionSpec as P

BOTH = ("dom", "band")
BF16 = jnp.bfloat16
F32 = jnp.float32
CELL_PAD = 128
MIB = 1 << 20


def spec(space=pltpu.VMEM):
    return pl.BlockSpec(memory_space=space)


def nn(a, b):
    return lax.dot_general(a, b, (((1,), (0,)), ((), ())), preferred_element_type=F32)


def nt(a, b):
    return lax.dot_general(a, b, (((1,), (1,)), ((), ())), preferred_element_type=F32)


def one_hot(rows, row):
    hit = lax.broadcasted_iota(row.dtype, (rows, row.shape[1]), 0) == row
    return hit.astype(F32).astype(BF16)


def pair_mask(column, row):
    return (column == row).astype(F32).astype(BF16)


def send_body(parts, part_ref, block_ref, lists_ref, left_ref, right_ref):
    own = block_ref.shape[1]
    states = block_ref.shape[0]
    lists = lists_ref[...]
    slots = lists.shape[1]
    part = lax.broadcasted_iota(jnp.int32, (16, slots), 0)
    codes = jnp.where(part == 4, 1, 0)
    for side, end in ((0, 0), (1, parts - 1)):
        one = lists[side : side + 1]
        codes = jnp.where(part == 2 * side, (one >> 5) + jnp.where(part_ref[0] == end, 128, 0), codes)
        codes = jnp.where(part == 2 * side + 1, one & 31, codes)
    codes = codes.astype(F32).astype(BF16)
    for side, out in ((0, left_ref), (1, right_ref)):
        out[0:states, :] = nn(block_ref[...], one_hot(own, lists[side : side + 1])).astype(BF16)
        out[states : states + 16, :] = codes


def send_first(parts, part, block, lists):
    states, slots = block.shape[0], lists.shape[1]
    shape = jax.ShapeDtypeStruct((states + 16, slots), BF16)
    return pl.pallas_call(
        lambda *refs: send_body(parts, *refs),
        out_shape=(shape, shape),
        in_specs=[spec(pltpu.SMEM)] + [spec()] * 2,
        out_specs=(spec(), spec()),
        name="send_first",
    )(part, block, lists)


def build_body(band_ref, packed_ref, out_ref, hot, left):
    half, full = out_ref.shape
    cells = left.shape[1] // CELL_PAD
    first = band_ref[0] * half
    matrix = packed_ref[cells : cells + CELL_PAD, :].T
    nothing = jnp.zeros((CELL_PAD, CELL_PAD), F32)
    pair_matrix = jnp.concatenate(
        [jnp.concatenate([matrix, nothing], axis=1), jnp.concatenate([nothing, matrix], axis=1)], axis=0
    ).astype(BF16)
    for pair in range(cells // 2):
        both = (2 * pair, 2 * pair + 1)
        row = jnp.concatenate([packed_ref[c : c + 1, :] for c in both], axis=1).astype(jnp.int32)
        at = cells + CELL_PAD
        gain = [jnp.broadcast_to(packed_ref[at : at + 1, c : c + 1], (1, CELL_PAD)) for c in both]
        cols = slice(pair * 2 * CELL_PAD, (pair + 1) * 2 * CELL_PAD)
        product = nn(one_hot(half, row - first), pair_matrix)
        left[:, cols] = (product * jnp.concatenate(gain, axis=1)).astype(BF16)
        hot[:, cols] = one_hot(full, row)
    for at in range(0, half, 256):
        out_ref[at : at + 256, :] = nt(left[at : at + 256, :], hot[...]).astype(BF16)


def build(band, cell_nodes, cell_matrix, cell_scale, full):
    cells, nodes = cell_nodes.shape
    half = full // 2
    entries = cells * CELL_PAD
    spare = CELL_PAD - nodes
    packed = jnp.concatenate(
        [
            jnp.pad(cell_nodes.astype(F32), ((0, 0), (0, spare)), constant_values=-8192.0),
            jnp.pad(cell_matrix.astype(F32), ((0, spare), (0, spare))),
            jnp.pad(cell_scale[None], ((0, 7), (0, CELL_PAD - cells))),
        ],
        axis=0,
    )
    return pl.pallas_call(
        build_body,
        out_shape=jax.ShapeDtypeStruct((half, full), BF16),
        in_specs=[spec(pltpu.SMEM), spec()],
        out_specs=spec(),
        scratch_shapes=[pltpu.VMEM((full, entries), BF16), pltpu.VMEM((half, entries), BF16)],
        compiler_params=pltpu.CompilerParams(vmem_limit_bytes=26 * MIB),
        cost_estimate=pl.CostEstimate(
            flops=2 * half * entries * full, bytes_accessed=2 * half * full, transcendentals=0
        ),
        name="build",
    )(band, packed)


def decode(codes_ref):
    slots = codes_ref.shape[1]
    codes = codes_ref[codes_ref.shape[0] - 16 :, :].astype(F32)
    rows = [codes[2 * s : 2 * s + 1] * 32.0 + codes[2 * s + 1 : 2 * s + 2] for s in (0, 1)]
    part = lax.broadcasted_iota(jnp.int32, (8, slots), 0)
    both = jnp.where(part == 0, rows[0], rows[1])
    columns = both.T + (1.0 - codes[4:5, 0:1]) * 16384.0
    return rows, [columns[:, 0:1], columns[:, 1:2]]


def assemble(partial_ref, ghost_ref, got_ref, lists, from_left_ref, from_right_ref, own):
    slots = lists.shape[1]
    (left_rows, left_cols), (right_rows, right_cols) = decode(from_left_ref), decode(from_right_ref)
    ghost = ghost_ref[...]
    ghost_left, ghost_right = ghost[:, 0:slots], ghost[:, slots : 2 * slots]
    states = ghost.shape[0]
    got_left, got_right = got_ref[0:states, :], got_ref[states : 2 * states, :]
    near_left, near_right = got_left[:, 0:slots], got_right[:, 0:slots]
    whole_own = (
        partial_ref[...]
        + nt(near_left, one_hot(own, lists[0:1]))
        + nt(near_right, one_hot(own, lists[1:2]))
    )
    whole_left = (
        got_left[:, slots : 2 * slots].astype(F32)
        + nn(got_left[:, 2 * slots : 3 * slots], pair_mask(left_cols[0], left_rows[1]))
        + nn(ghost_left, pair_mask(left_cols[1], left_rows[1]))
    )
    whole_right = (
        got_right[:, slots : 2 * slots].astype(F32)
        + nn(got_right[:, 2 * slots : 3 * slots], pair_mask(right_cols[1], right_rows[0]))
        + nn(ghost_right, pair_mask(right_cols[0], right_rows[0]))
    )
    return whole_own, whole_left, whole_right


def times_half(which, x_ref, w_ref, cols):
    half = w_ref.shape[0]
    return nn(x_ref[:, pl.ds(pl.multiple_of(which * half, 128), half)], w_ref[:, cols])


def times_operator(band, x_ref, mine_ref, other_ref, cols):
    return times_half(band, x_ref, mine_ref, cols) + times_half(1 - band, x_ref, other_ref, cols)


def apply_body(band_ref, x_ref, mine_ref, other_ref, *refs):
    give(band_ref, times_operator(band_ref[0], x_ref, mine_ref, other_ref, slice(None)), x_ref, *refs)


def give(band_ref, result, x_ref, potential_ref, lists, partial_out, ghost_out, near_out, far_out):
    own = partial_out.shape[1]
    slots = lists.shape[1]
    partial = result[:, 0:own] + potential_ref[...] * x_ref[:, 0:own].astype(F32)
    partial_out[...] = partial
    ghost = result[:, own:].astype(BF16)
    ghost_out[...] = ghost
    right = band_ref[0] == 1
    mine = jnp.where(right, lists[1:2], lists[0:1])
    edge = jnp.where(right, ghost[:, slots : 2 * slots], ghost[:, 0:slots])
    near_out[:, 0:slots] = edge
    near_out[:, slots : 2 * slots] = nn(partial.astype(BF16), one_hot(own, mine)).astype(BF16)
    far_out[...] = edge


def first_body(
    band_ref, mine_ref, other_hbm, potential_ref, lists_ref, x_ref, other_out, partial_out, ghost_out, near_out,
    far_out, sem,
):
    piece = other_out.shape[0] // 4
    arrivals = [
        pltpu.make_async_copy(other_hbm.at[i * piece : (i + 1) * piece], other_out.at[i * piece : (i + 1) * piece], sem.at[i])
        for i in range(4)
    ]
    for arrival in arrivals:
        arrival.start()
    result = times_half(band_ref[0], x_ref, mine_ref, slice(None))
    for arrival in arrivals:
        arrival.wait()
    result = result + times_half(1 - band_ref[0], x_ref, other_out, slice(None))
    give(band_ref, result, x_ref, potential_ref, lists_ref[...], partial_out, ghost_out, near_out, far_out)


def new_states(older_ref, x_out, pieces):
    own = pieces[0].shape[1]
    slots = pieces[1].shape[1]
    at = 0
    for piece in pieces:
        cols = slice(at, at + piece.shape[1])
        if older_ref is not None:
            piece = 2.0 * piece - older_ref[:, cols].astype(F32)
        x_out[:, cols] = piece.astype(BF16)
        at += piece.shape[1]


def next_body(chebyshev, *refs):
    band_ref, mine_ref, other_ref, potential_ref, lists_ref, fl_ref, fr_ref, partial_ref, ghost_ref, got_ref = refs[:10]
    older_ref = refs[10] if chebyshev else None
    rest = refs[11:] if chebyshev else refs[10:]
    x_out, outs = (rest[-1], rest[:-1]) if chebyshev else (rest[0], rest[1:])
    lists = lists_ref[...]
    own = partial_ref.shape[1]
    new_states(older_ref, x_out, assemble(partial_ref, ghost_ref, got_ref, lists, fl_ref, fr_ref, own))
    apply_body(band_ref, x_out, mine_ref, other_ref, potential_ref, lists, *outs)


def last_body(
    band_ref, mine_ref, other_ref, potential_ref, lists_ref, fl_ref, fr_ref, partial_ref, ghost_ref, got_ref,
    older_ref, own_out, sums_out, x_all, pot,
):
    lists = lists_ref[...]
    own = partial_ref.shape[1]
    states = partial_ref.shape[0]
    slots = lists.shape[1]
    new_states(older_ref, x_all, assemble(partial_ref, ghost_ref, got_ref, lists, fl_ref, fr_ref, own))
    pot[...] = potential_ref[...]
    half = own // 2
    mine = pl.ds(pl.multiple_of(band_ref[0] * half, 128), half)
    edge = pl.ds(pl.multiple_of(own + band_ref[0] * slots, 128), slots)
    x_mine = x_all[:, mine]
    own_out[...] = x_mine
    sums_out[0:states, :] = nt(x_mine, x_mine)
    image = times_operator(band_ref[0], x_all, mine_ref, other_ref, mine) + pot[:, mine] * x_mine.astype(F32)
    image_edge = times_operator(band_ref[0], x_all, mine_ref, other_ref, edge)
    sums_out[states : 2 * states, :] = nt(x_mine, image.astype(BF16)) + nt(x_all[:, edge], image_edge.astype(BF16))


def apply_shapes(states, own, slots):
    return (
        jax.ShapeDtypeStruct((states, own), F32),
        jax.ShapeDtypeStruct((states, 2 * slots), BF16),
        jax.ShapeDtypeStruct((states, 2 * slots), BF16),
        jax.ShapeDtypeStruct((states, slots), BF16),
    )


def stage_call(body, args, shapes, name, scratch=(), anywhere=()):
    return pl.pallas_call(
        body,
        out_shape=tuple(shapes),
        in_specs=[spec(pltpu.SMEM)] + [spec(pl.ANY if i in anywhere else pltpu.VMEM) for i in range(1, len(args))],
        out_specs=tuple(spec() for _ in shapes),
        scratch_shapes=list(scratch),
        compiler_params=pltpu.CompilerParams(vmem_limit_bytes=16 * MIB),
        name=name,
    )(*args)


def shift(x, axis, by):
    devices = lax.axis_size(axis)
    return lax.ppermute(x, axis, [(i, i + by) for i in range(devices) if 0 <= i + by < devices])


def across(x, by):
    parts = lax.axis_size("dom")
    pairs = [(2 * d + 1, 2 * (d + by)) for d in range(parts - by)]
    pairs += [(2 * (d + by), 2 * d + 1) for d in range(parts - by)]
    return lax.ppermute(x, BOTH, pairs)


def far_groups(parts):
    pairs = [[2 * d + 1, 2 * d + 4] for d in range(parts - 2)]
    return pairs + [[0, 2], [2 * parts - 3, 2 * parts - 1]]


def exchange(band, near, far):
    rows = far.shape[0]
    near = across(near, 1)
    both = lax.all_gather(far, BOTH, axis_index_groups=far_groups(lax.axis_size("dom")), axis=0, tiled=True)
    far = lax.dynamic_slice_in_dim(both, band * rows, rows, 0)
    return lax.all_gather(jnp.concatenate([near, far], axis=1), "band", axis=0, tiled=True)


def group_lists():
    planes, along_z = {}, {}
    for x in range(4):
        for z in range(16):
            for y in range(4):
                for b in range(2):
                    i = ((x * 16 + z) * 4 + y) * 2 + b
                    planes.setdefault(z, []).append(i)
                    along_z.setdefault((x, y, b), []).append(i)
    return list(planes.values()), list(along_z.values())


def swap_pieces(x, groups):
    return lax.all_to_all(x, BOTH, 0, 0, axis_index_groups=groups, tiled=True)


def copies(piece, count):
    return jnp.broadcast_to(piece[None], (count,) + piece.shape).reshape(count * piece.shape[0], piece.shape[1])


def sum_pieces(x, count):
    return x.reshape(count, x.shape[0] // count, x.shape[1]).sum(0)


def sum_everywhere(x):
    planes, along_z = group_lists()
    in_plane, depth = len(planes[0]), len(along_z[0])
    piece = sum_pieces(swap_pieces(x, planes), in_plane)
    piece = sum_pieces(swap_pieces(copies(piece, depth), along_z), depth)
    return swap_pieces(copies(piece, in_plane), planes)


def exact(a, b):
    return jnp.dot(a, b, precision=lax.Precision.HIGHEST, preferred_element_type=F32)


def weighted(weights, rows):
    total = None
    for w, r in zip(weights, rows):
        total = w * r if total is None else total + w * r
    return total


def stack(rows):
    part = lax.broadcasted_iota(jnp.int32, rows[0].shape, 0)
    out = rows[0]
    for i in range(1, len(rows)):
        out = jnp.where(part == i, rows[i], out)
    return out


def inverse_of_eight(panel, first):
    wide = panel.shape
    columns = [jnp.broadcast_to(panel[:, first + j : first + j + 1], wide) for j in range(8)]
    low = {(i, j): jnp.broadcast_to(columns[j][i : i + 1, :], wide) for j in range(8) for i in range(j, 8)}
    inv = {}
    for j in range(8):
        inv[j, j] = lax.rsqrt(low[j, j])
        for i in range(j + 1, 8):
            low[i, j] = low[i, j] * inv[j, j]
        for k in range(j + 1, 8):
            for i in range(k, 8):
                low[i, k] = low[i, k] - low[i, j] * low[k, j]
        for k in range(j):
            inv[j, k] = -inv[j, j] * weighted([low[j, m] for m in range(k, j)], [inv[m, k] for m in range(k, j)])
    return inv


def finish_body(scale, total_ref, own_ref, ortho_out, projected_out, inverse_ref):
    size = total_ref.shape[1]
    block = 32
    schur = total_ref[0:size, :] * scale
    at = lax.broadcasted_iota(jnp.int32, (size, size), 0)
    beside = (at == lax.broadcasted_iota(jnp.int32, (size, size), 1)).astype(F32)
    for start in range(0, size, block):
        here = [schur[i : i + 8] for i in range(0, block, 8)]
        here_beside = [beside[i : i + 8] for i in range(0, block, 8)]
        done, done_beside = [], []
        for p in range(block // 8):
            first = start + 8 * p
            top, top_beside = here[p], here_beside[p]
            inv = inverse_of_eight(top, first)
            rows = [jnp.broadcast_to(top[i : i + 1], top.shape) for i in range(8)]
            rows_beside = [jnp.broadcast_to(top_beside[i : i + 1], top.shape) for i in range(8)]
            solved = [weighted([inv[i, k] for k in range(i + 1)], rows) for i in range(8)]
            solved_beside = [weighted([inv[i, k] for k in range(i + 1)], rows_beside) for i in range(8)]
            done.append(stack(solved))
            done_beside.append(stack(solved_beside))
            inverse_ref[first : first + 8, :] = done_beside[-1]
            if p + 1 < block // 8:
                twice = [weighted([inv[k, i] for k in range(i, 8)], solved[i:]) for i in range(8)]
                twice_beside = [weighted([inv[k, i] for k in range(i, 8)], solved_beside[i:]) for i in range(8)]
            for q in range(p + 1, block // 8):
                columns = [jnp.broadcast_to(here[q][:, first + j : first + j + 1], top.shape) for j in range(8)]
                here[q] = here[q] - weighted(columns, twice)
                here_beside[q] = here_beside[q] - weighted(columns, twice_beside)
        if start + block < size:
            solved = jnp.concatenate(done, axis=0)
            both = jnp.concatenate([solved, jnp.concatenate(done_beside, axis=0)], axis=1)
            taken = exact(solved.T[start + block :], both)
            schur = schur[block:] - taken[:, 0:size]
            beside = beside[block:] - taken[:, size:]
    inverse = inverse_ref[...]
    coarse = inverse.astype(BF16)
    rest = inverse - coarse.astype(F32)
    fine = rest.astype(BF16)
    finest = (rest - fine.astype(F32)).astype(BF16)
    own = own_ref[...]
    ortho_out[...] = nn(coarse, own) + (nn(fine, own) + nn(finest, own))
    half_solved = exact(inverse, total_ref[size : 2 * size, :] * scale)
    projected_out[...] = lax.dot_general(
        half_solved, inverse, (((1,), (1,)), ((), ())), precision=lax.Precision.HIGHEST, preferred_element_type=F32
    )


def finish(scale, total, own_part):
    states, nodes = own_part.shape
    return pl.pallas_call(
        lambda *refs: finish_body(scale, *refs),
        out_shape=(jax.ShapeDtypeStruct((states, nodes), F32), jax.ShapeDtypeStruct((states, states), F32)),
        in_specs=[spec()] * 2,
        out_specs=(spec(), spec()),
        scratch_shapes=[pltpu.VMEM((states, states), F32)],
        compiler_params=pltpu.CompilerParams(vmem_limit_bytes=16 * MIB),
        name="finish",
    )(total, own_part)


def shards(block, cell_nodes, send_lists, cell_matrix, cell_scale, potential):
    lists = send_lists[0]
    own, slots = block.shape[1], lists.shape[1]
    full = own + 2 * slots
    states_here = block.shape[0]
    states = 2 * states_here
    core = lax.axis_index("band")
    band = core.astype(jnp.int32).reshape(1)
    part = lax.axis_index("dom").astype(jnp.int32).reshape(1)
    potential = potential.reshape(1, own)

    to_left, to_right = send_first(lax.axis_size("dom"), part, block, lists)
    to_left, to_right, cell_nodes = lax.optimization_barrier((to_left, to_right, cell_nodes))
    from_left = shift(to_right, "dom", 1)
    from_right = shift(to_left, "dom", -1)
    mine = build(band, cell_nodes, cell_matrix, cell_scale, full)
    mine, from_left, from_right = lax.optimization_barrier((mine, from_left, from_right))
    other = lax.ppermute(mine, "band", [(0, 1), (1, 0)])
    x_here = jnp.concatenate([block, from_left[:states_here], from_right[:states_here]], axis=1)
    x0 = lax.all_gather(x_here, "band", axis=0, tiled=True)

    shapes = apply_shapes(states, own, slots)
    x_shape = jax.ShapeDtypeStruct((states, full), BF16)
    fixed = (band, mine, other, potential, lists)
    ends = fixed + (from_left, from_right)
    other_shape = jax.ShapeDtypeStruct(other.shape, other.dtype)
    other, partial, ghost, near, far = stage_call(
        first_body, fixed + (x0,), (other_shape,) + shapes, "apply_one", (pltpu.SemaphoreType.DMA((4,)),), (2,)
    )
    fixed = (band, mine, other, potential, lists)
    ends = fixed + (from_left, from_right)
    got = exchange(core, near, far)
    x1, partial, ghost, near, far = stage_call(
        lambda *r: next_body(False, *r), ends + (partial, ghost, got), (x_shape,) + shapes, "apply_two"
    )
    got = exchange(core, near, far)
    partial, ghost, near, far = stage_call(
        lambda *r: next_body(True, *r),
        ends + (partial, ghost, got, x0),
        shapes,
        "apply_three",
        (pltpu.VMEM((states, full), BF16),),
    )
    got = exchange(core, near, far)
    own_part, sums = stage_call(
        last_body,
        ends + (partial, ghost, got, x1),
        (jax.ShapeDtypeStruct((states, own // 2), BF16), jax.ShapeDtypeStruct((2 * states, states), F32)),
        "apply_four",
        (pltpu.VMEM((states, full), BF16), pltpu.VMEM((1, own), F32)),
    )
    return finish(1.0 / (own * lax.axis_size("dom")), sum_everywhere(sums), own_part)


def solution(mesh):
    return jax.shard_map(
        shards,
        mesh=mesh,
        in_specs=(P("band", "dom"), P("dom", None), P("dom", None, None), P(), P("dom"), P("dom")),
        out_specs=(P(None, ("dom", "band")), P()),
        check_vma=False,
    )
```
